512 devices in a mesh: dp: 2 (over y_lo), tm: 8 (over x, core), space: 32 (over y_hi, z).
Axes of the slice: x: 4, y: 4 (y_hi: 2, y_lo: 2; y = y_hi * 2 + y_lo), z: 16, core: 2. Of those that a mesh axis runs over, the one named last changes fastest.
Arguments:
- inputs: bfloat16 [2, 16, 64, 64, 256], P('dp', 'tm', 'space'), may hold values from -6 to 6
- cotangent: bfloat16 [2, 32, 128, 128, 128], P('dp', 'tm', 'space'), may hold values from -6 to 6
- spatial_weight: bfloat16 [3, 3, 256, 256], replicated, may hold values from -0.125 to 0.125
- time_weight: bfloat16 [3, 256, 256], replicated, may hold values from -0.21875 to 0.21875
- up_weight: bfloat16 [256, 1024], replicated, may hold values from -0.375 to 0.375
Outputs:
- input_grad: bfloat16 [2, 16, 64, 64, 256], P('dp', 'tm', 'space')
- spatial_grad: float32 [3, 3, 256, 256], P(None, None, None, 'space')
- time_grad: float32 [3, 256, 256], P(None, None, 'space')
- up_grad: float32 [256, 1024], P(None, 'space')
The draws below stay inside these ranges and needn't reach their ends.
All inputs are finite; a program needn't handle non-finite values.
Results may differ from the reference program's by a relative error of at most 0.0051.
Values may be sent and summed in bfloat16 or wider, within the bound.
No kernel may reach another device: no remote copies, remote signals or barrier semaphores. Data moves between devices by JAX's collectives and lax.ppermute only.
A program may use at most 64 MiB of HBM per device.

```python
import jax
import jax.numpy as jnp
from jax import lax

C = 256
CO = 128
W = 64
CLIPS = 2
FRAMES = 16
ROWS = 64


def strengthened(entries, key, source, target, parts, factor):
    def block_of(axis_at):
        return (jnp.arange(entries.shape[axis_at]) // (entries.shape[axis_at] // parts)).reshape((-1,) + (1,) * (entries.ndim - 1 - axis_at))

    near = jax.random.permutation(key, parts)[block_of(target)]
    other_side = (block_of(target) + parts // 2) % parts
    return jnp.where((block_of(source) == near) | (block_of(source) == other_side), factor * entries, entries)


def shard_levels(key, dims, shards, low, high):
    loudness = 1.0
    for dim, shards_of in shards:
        draws = jax.random.uniform(jax.random.fold_in(jax.random.fold_in(key, 6), dim), (shards_of,), jnp.float32, low / len(shards), high / len(shards))
        loudness = loudness * jnp.repeat(jnp.exp(draws), dims[dim] // shards_of).reshape((-1,) + (1,) * (len(dims) - 1 - dim))
    return loudness


def centred(own_key, extent, width, most, pieces=(), held_as=jnp.bfloat16):
    level = shard_levels(own_key, extent, pieces, -0.22, 0.18) if pieces else 1.0
    array = jax.random.normal(own_key, extent, jnp.float32) * width * level
    return jnp.minimum(jnp.maximum(array, -most), most).astype(held_as)


def gaussian_with(own_key, dims, scale, limit, split, heavy, dtype=jnp.bfloat16):
    drawn = scale * jax.random.normal(own_key, dims, jnp.float32)
    if split:
        drawn = drawn * shard_levels(own_key, dims, split, -0.22, 0.18)
    return jnp.clip(strengthened(drawn, jax.random.fold_in(own_key, 3), *heavy), -limit, limit).astype(dtype)


def setup_inputs(seed: int = 0) -> dict:
    splits = jax.random.split(jax.random.key(seed), 6)
    inputs = centred(splits[0], (CLIPS, FRAMES, ROWS, W, C), 1.0, 6.0, ((0, 2), (1, 8), (2, 32)))
    cotangent = gaussian_with(splits[1], (CLIPS, 2 * FRAMES, 2 * ROWS, 2 * W, CO), 1.0, 6.0, ((0, 2), (1, 8), (2, 32)), (2, 4, 32, 2.75))
    spatial_weight = centred(splits[2], (3, 3, C, C), (9 * C) ** -0.5, 0.125)
    time_weight = centred(splits[3], (3, C, C), (3 * C) ** -0.5, 0.21875)
    up_weight = centred(splits[4], (C, 8 * CO), C ** -0.5, 0.375)
    return dict(inputs=inputs, cotangent=cotangent, spatial_weight=spatial_weight, time_weight=time_weight, up_weight=up_weight)


epsilon = 1e-06

def spatial(padded, weight, height, breadth):
    summed = None
    for row_tap in range(3):
        for col_tap in range(3):
            window = padded[:, :, row_tap:row_tap + height, col_tap:col_tap + breadth, :]
            product = jnp.dot(window.reshape(-1, window.shape[-1]), weight[row_tap, col_tap], preferred_element_type=jnp.float32)
            summed = product if summed is None else summed + product
    return summed.reshape(padded.shape[:2] + (height, breadth, weight.shape[-1]))

def filter_grad(padded, grads_in, height, breadth):
    flattened = grads_in.reshape(-1, grads_in.shape[-1])
    collected = []
    for row_tap in range(3):
        across = []
        for col_tap in range(3):
            window = padded[:, :, row_tap:row_tap + height, col_tap:col_tap + breadth, :]
            across.append(lax.dot_general(window.reshape(-1, window.shape[-1]), flattened, (((0,), (0,)), ((), ())), preferred_element_type=jnp.float32))
        collected.append(jnp.stack(across))
    return jnp.stack(collected)

def along_time(padded, weight, frames, starts):
    summed = None
    for time_tap in range(3):
        window = padded[:, starts[time_tap]:starts[time_tap] + frames]
        product = jnp.dot(window.reshape(-1, window.shape[-1]), weight[time_tap], preferred_element_type=jnp.float32)
        summed = product if summed is None else summed + product
    return summed.reshape(padded.shape[:1] + (frames,) + padded.shape[2:4] + (weight.shape[-1],))

def reference(inputs, cotangent, spatial_weight, time_weight, up_weight):
    clip_count, frames, height, breadth, channels = inputs.shape
    input_rim = jnp.pad(inputs, ((0, 0), (0, 0), (1, 1), (1, 1), (0, 0)))
    pre_act = spatial(input_rim, spatial_weight, height, breadth)
    rms_scale = jnp.sqrt(lax.optimization_barrier(jnp.mean(pre_act * pre_act, -1, keepdims=True)) + epsilon)
    normed = pre_act / rms_scale
    activated = jax.nn.silu(normed).astype(jnp.bfloat16)
    act_window = jnp.pad(activated, ((0, 0), (2, 0), (0, 0), (0, 0), (0, 0)))
    mixed_time = along_time(act_window, time_weight, frames, (2, 1, 0))
    summed_state = (inputs.astype(jnp.float32) + mixed_time).astype(jnp.bfloat16)
    upward = cotangent.reshape(clip_count, frames, 2, height, 2, breadth, 2, -1)
    upward = upward.transpose(0, 1, 3, 5, 2, 4, 6, 7).reshape(clip_count, frames, height, breadth, -1)
    flat_up = upward.reshape(-1, upward.shape[-1])
    state_grad = lax.dot_general(flat_up, up_weight, (((1,), (1,)), ((), ())), preferred_element_type=jnp.float32).reshape(inputs.shape)
    up_grad = lax.dot_general(summed_state.reshape(-1, channels), flat_up, (((0,), (0,)), ((), ())), preferred_element_type=jnp.float32)
    time_cot = state_grad.astype(jnp.bfloat16)
    flat_cot = time_cot.reshape(-1, channels)
    time_grad = jnp.stack([lax.dot_general(act_window[:, 2 - time_tap:2 - time_tap + frames].reshape(-1, channels), flat_cot, (((0,), (0,)), ((), ())), preferred_element_type=jnp.float32) for time_tap in range(3)])
    later_cot = jnp.pad(time_cot, ((0, 0), (0, 2), (0, 0), (0, 0), (0, 0)))
    act_grad = along_time(later_cot, jnp.swapaxes(time_weight, 1, 2), frames, (0, 1, 2))
    sigmoid_part = jax.nn.sigmoid(normed)
    norm_grad = act_grad * sigmoid_part * (1.0 + normed * (1.0 - sigmoid_part))
    pre_grad = ((norm_grad - normed * lax.optimization_barrier(jnp.mean(norm_grad * normed, -1, keepdims=True))) / rms_scale).astype(jnp.bfloat16)
    grad_window = jnp.pad(pre_grad, ((0, 0), (0, 0), (1, 1), (1, 1), (0, 0)))
    spatial_grad = filter_grad(input_rim, pre_grad, height, breadth)
    flipped = jnp.swapaxes(spatial_weight[::-1, ::-1], 2, 3)
    input_grad = (state_grad + spatial(grad_window, flipped, height, breadth)).astype(jnp.bfloat16)
    return (input_grad, spatial_grad, time_grad, up_grad)
```

```python
import jax
import jax.numpy as jnp
from jax import lax
from jax.sharding import PartitionSpec as P

epsilon = 1e-06


def with_halo(block, sides, width):
    for axis, dim in sides:
        count = lax.axis_size(axis)
        forward = [(i, i + 1) for i in range(count - 1)]
        backward = [(target, source) for source, target in forward]
        low = lax.ppermute(
            lax.slice_in_dim(block, block.shape[dim] - width, None, axis=dim), axis, forward
        )
        high = lax.ppermute(lax.slice_in_dim(block, 0, width, axis=dim), axis, backward)
        block = jnp.concatenate([low, block, high], axis=dim)
    return block


def from_behind(value, axis, steps):
    count = lax.axis_size(axis)
    first, last = (max(0, -steps), min(count, count - steps))
    return lax.ppermute(value, axis, [(source, source + steps) for source in range(first, last)])


def spatial(padded, weight, height, breadth):
    summed = None
    for row_tap in range(3):
        for col_tap in range(3):
            window = padded[:, :, row_tap : row_tap + height, col_tap : col_tap + breadth, :]
            product = jnp.dot(
                window.reshape(-1, window.shape[-1]),
                weight[row_tap, col_tap],
                preferred_element_type=jnp.float32,
            )
            summed = product if summed is None else summed + product
    return summed.reshape(padded.shape[:2] + (height, breadth, weight.shape[-1]))


def filter_grad(padded, grads_in, height, breadth):
    flattened = grads_in.reshape(-1, grads_in.shape[-1])
    collected = []
    for row_tap in range(3):
        across = []
        for col_tap in range(3):
            window = padded[:, :, row_tap : row_tap + height, col_tap : col_tap + breadth, :]
            across.append(
                lax.dot_general(
                    flattened,
                    window.reshape(-1, window.shape[-1]),
                    (((0,), (0,)), ((), ())),
                    preferred_element_type=jnp.float32,
                )
            )
        collected.append(jnp.stack(across))
    return jnp.stack(collected)


def along_time(padded, weight, frames, starts):
    summed = None
    for time_tap in range(3):
        window = padded[:, starts[time_tap] : starts[time_tap] + frames]
        product = jnp.dot(
            window.reshape(-1, window.shape[-1]),
            weight[time_tap],
            preferred_element_type=jnp.float32,
        )
        summed = product if summed is None else summed + product
    return summed.reshape(padded.shape[:1] + (frames,) + padded.shape[2:4] + (weight.shape[-1],))


def reduced(spatial_grad, time_grad, up_grad):
    pieces = lax.axis_size("space")
    group = ("dp", "tm")
    members = lax.axis_size("dp") * lax.axis_size("tm")
    channels = spatial_grad.shape[-1]
    share = channels // pieces
    taps = jnp.concatenate((spatial_grad.reshape(9, channels, channels), time_grad), axis=0)
    taps = taps.reshape(12, pieces, share, channels).transpose(1, 0, 2, 3)
    rows = jnp.concatenate(
        (taps.reshape(pieces, 12 * share, channels), up_grad.reshape(pieces, -1, channels)), axis=1
    )
    blocks = members // 2
    rows = rows.astype(jnp.bfloat16).reshape(pieces, blocks, -1, 2, channels // 2)
    rows = rows.transpose(1, 3, 0, 2, 4).reshape(members, pieces, -1, channels // 2)
    first = lax.all_to_all(rows, group, 0, 0)
    first = jnp.sum(first.astype(jnp.float32), axis=0).astype(jnp.bfloat16)
    second = lax.all_to_all(first, "space", 0, 0)
    second = jnp.sum(second.astype(jnp.float32), axis=0)
    whole = lax.all_gather(second, group)
    whole = whole.reshape(blocks, 2, -1, channels // 2).transpose(0, 2, 1, 3).reshape(-1, channels)
    split = 12 * share
    tap_out = jnp.swapaxes(whole[:split].reshape(12, share, channels), 1, 2)
    return (
        tap_out[:9].reshape(3, 3, channels, share),
        tap_out[9:],
        jnp.swapaxes(whole[split:], 0, 1),
    )


def local(inputs, cotangent, spatial_weight, time_weight, up_weight):
    clip_count, frames, height, breadth, channels = inputs.shape
    rimmed = with_halo(inputs, (("space", 2),), 1)
    input_rim = jnp.pad(rimmed, ((0, 0), (0, 0), (0, 0), (1, 1), (0, 0)))
    pre_act = spatial(input_rim, spatial_weight, height, breadth)
    rms_scale = jnp.sqrt(jnp.mean(pre_act * pre_act, -1, keepdims=True) + epsilon)
    normed = pre_act / rms_scale
    activated = jax.nn.silu(normed).astype(jnp.bfloat16)
    earlier = from_behind(activated, "tm", 1)
    act_window = jnp.concatenate((earlier, activated), axis=1)
    mixed_time = along_time(act_window, time_weight, frames, (2, 1, 0))
    summed_state = (inputs.astype(jnp.float32) + mixed_time).astype(jnp.bfloat16)
    upward = cotangent.reshape(clip_count, frames, 2, height, 2, breadth, 2, -1)
    upward = upward.transpose(0, 1, 3, 5, 2, 4, 6, 7).reshape(
        clip_count, frames, height, breadth, -1
    )
    flat_up = upward.reshape(-1, upward.shape[-1])
    state_grad = lax.dot_general(
        flat_up, up_weight, (((1,), (1,)), ((), ())), preferred_element_type=jnp.float32
    ).reshape(inputs.shape)
    up_grad = lax.dot_general(
        flat_up,
        summed_state.reshape(-1, channels),
        (((0,), (0,)), ((), ())),
        preferred_element_type=jnp.float32,
    )
    time_cot = state_grad.astype(jnp.bfloat16)
    flat_cot = time_cot.reshape(-1, channels)
    time_grad = jnp.stack(
        [
            lax.dot_general(
                flat_cot,
                act_window[:, 2 - time_tap : 2 - time_tap + frames].reshape(-1, channels),
                (((0,), (0,)), ((), ())),
                preferred_element_type=jnp.float32,
            )
            for time_tap in range(3)
        ]
    )
    following = from_behind(time_cot, "tm", -1)
    later_cot = jnp.concatenate((time_cot, following), axis=1)
    act_grad = along_time(later_cot, jnp.swapaxes(time_weight, 1, 2), frames, (0, 1, 2))
    sigmoid_part = jax.nn.sigmoid(normed)
    norm_grad = act_grad * sigmoid_part * (1.0 + normed * (1.0 - sigmoid_part))
    pre_grad = (
        (norm_grad - normed * jnp.mean(norm_grad * normed, -1, keepdims=True)) / rms_scale
    ).astype(jnp.bfloat16)
    grad_rimmed = with_halo(pre_grad, (("space", 2),), 1)
    grad_window = jnp.pad(grad_rimmed, ((0, 0), (0, 0), (0, 0), (1, 1), (0, 0)))
    spatial_grad = filter_grad(input_rim, pre_grad, height, breadth)
    flipped = jnp.swapaxes(spatial_weight[::-1, ::-1], 2, 3)
    input_grad = (state_grad + spatial(grad_window, flipped, height, breadth)).astype(jnp.bfloat16)
    spatial_out, time_out, up_out = reduced(spatial_grad, time_grad, up_grad)
    return (input_grad, spatial_out, time_out, up_out)


def solution(mesh):
    return jax.shard_map(
        local,
        mesh=mesh,
        in_specs=(
            P("dp", "tm", "space", None, None),
            P("dp", "tm", "space", None, None),
            P(),
            P(),
            P(),
        ),
        out_specs=(
            P("dp", "tm", "space", None, None),
            P(None, None, None, "space"),
            P(None, None, "space"),
            P(None, "space"),
        ),
        check_vma=False,
    )
```

```python
import jax
import jax.numpy as jnp
from jax import lax
from jax.sharding import Mesh, PartitionSpec as P

epsilon = 1e-06
TIME = ("x", "core")
SPACE = ("y_hi", "z_hi", "z_lo")


def with_halo(block, sides, width):
    for axis, dim in sides:
        count = 32
        forward = [(i, i + 1) for i in range(count - 1)]
        backward = [(target, source) for source, target in forward]
        low = lax.ppermute(
            lax.slice_in_dim(block, block.shape[dim] - width, None, axis=dim), axis, forward
        )
        high = lax.ppermute(lax.slice_in_dim(block, 0, width, axis=dim), axis, backward)
        block = jnp.concatenate([low, block, high], axis=dim)
    return block


def from_behind(value, axis, steps):
    count = 8
    first, last = (max(0, -steps), min(count, count - steps))
    return lax.ppermute(value, axis, [(source, source + steps) for source in range(first, last)])


def spatial(padded, weight, height, breadth):
    summed = None
    for row_tap in range(3):
        for col_tap in range(3):
            window = padded[:, :, row_tap : row_tap + height, col_tap : col_tap + breadth, :]
            product = jnp.dot(
                window.reshape(-1, window.shape[-1]),
                weight[row_tap, col_tap],
                preferred_element_type=jnp.float32,
            )
            summed = product if summed is None else summed + product
    return summed.reshape(padded.shape[:2] + (height, breadth, weight.shape[-1]))


def filter_grad(padded, grads_in, height, breadth):
    flattened = grads_in.reshape(-1, grads_in.shape[-1])
    collected = []
    for row_tap in range(3):
        across = []
        for col_tap in range(3):
            window = padded[:, :, row_tap : row_tap + height, col_tap : col_tap + breadth, :]
            across.append(
                lax.dot_general(
                    flattened,
                    window.reshape(-1, window.shape[-1]),
                    (((0,), (0,)), ((), ())),
                    preferred_element_type=jnp.float32,
                )
            )
        collected.append(jnp.stack(across))
    return jnp.stack(collected)


def along_time(padded, weight, frames, starts):
    summed = None
    for time_tap in range(3):
        window = padded[:, starts[time_tap] : starts[time_tap] + frames]
        product = jnp.dot(
            window.reshape(-1, window.shape[-1]),
            weight[time_tap],
            preferred_element_type=jnp.float32,
        )
        summed = product if summed is None else summed + product
    return summed.reshape(padded.shape[:1] + (frames,) + padded.shape[2:4] + (weight.shape[-1],))


def swapped(value, axes, sizes, flips):
    total = 1
    for size in sizes:
        total *= size
    pairs = []
    for source in range(total):
        rest, place, target = source, 1, 0
        for size, flip in zip(reversed(sizes), reversed(flips)):
            target += ((rest % size) ^ flip) * place
            rest //= size
            place *= size
        pairs.append((source, target))
    return lax.ppermute(value, axes, pairs)


def picked(choices, index):
    result = choices[0]
    for at in range(1, len(choices)):
        result = jnp.where(index == at, choices[at], result)
    return result


def reduced(spatial_grad, time_grad, up_grad):
    channels = spatial_grad.shape[-1]
    pieces = 32
    share = channels // pieces
    half = channels // 2
    taps = jnp.concatenate((spatial_grad.reshape(9, channels, channels), time_grad), axis=0)
    taps = taps.reshape(12, pieces, share, channels).transpose(1, 0, 2, 3)
    rows = jnp.concatenate(
        (taps.reshape(pieces, 12 * share, channels), up_grad.reshape(pieces, -1, channels)), axis=1
    )
    rows = rows.astype(jnp.bfloat16).reshape(pieces, 8, 16, 2, half).transpose(3, 1, 0, 2, 4)
    core = lax.axis_index("core")
    mine = jnp.where(core == 0, rows[0], rows[1])
    other = jnp.where(core == 0, rows[1], rows[0])
    arrived = swapped(other, ("core",), (2,), (1,))
    value = (mine.astype(jnp.float32) + arrived.astype(jnp.float32)).astype(jnp.bfloat16)
    value = lax.all_to_all(value, ("x", "y_lo"), 0, 0)
    value = jnp.sum(value.astype(jnp.float32), axis=0).astype(jnp.bfloat16)
    value = value.reshape(8, 4, 16, half)
    value = lax.all_to_all(value, ("y_hi", "z_hi"), 0, 0)
    value = jnp.sum(value.astype(jnp.float32), axis=0)
    value = lax.all_to_all(value, "z_lo", 0, 0)
    value = jnp.sum(value, axis=0)
    x = lax.axis_index("x")
    found = [value] + [swapped(value, ("x",), (4,), (flip,)) for flip in (1, 2, 3)]
    value = jnp.stack([picked(found, x ^ at) for at in range(4)])
    found = [value] + [
        swapped(value, ("y_lo", "core"), (2, 2), (flip // 2, flip % 2)) for flip in (1, 2, 3)
    ]
    y_core = lax.axis_index("y_lo") * 2 + core
    value = jnp.stack([picked(found, y_core ^ at) for at in range(4)])
    whole = value.reshape(2, 2, 4, 16, half).transpose(2, 0, 3, 1, 4).reshape(-1, channels)
    split = 12 * share
    tap_out = jnp.swapaxes(whole[:split].reshape(12, share, channels), 1, 2)
    return (
        tap_out[:9].reshape(3, 3, channels, share),
        tap_out[9:],
        jnp.swapaxes(whole[split:], 0, 1),
    )


def local(inputs, cotangent, spatial_weight, time_weight, up_weight):
    clip_count, frames, height, breadth, channels = inputs.shape
    rimmed = with_halo(inputs, ((SPACE, 2),), 1)
    input_rim = jnp.pad(rimmed, ((0, 0), (0, 0), (0, 0), (1, 1), (0, 0)))
    pre_act = spatial(input_rim, spatial_weight, height, breadth)
    rms_scale = jnp.sqrt(jnp.mean(pre_act * pre_act, -1, keepdims=True) + epsilon)
    normed = pre_act / rms_scale
    activated = jax.nn.silu(normed).astype(jnp.bfloat16)
    earlier = from_behind(activated, TIME, 1)
    act_window = jnp.concatenate((earlier, activated), axis=1)
    mixed_time = along_time(act_window, time_weight, frames, (2, 1, 0))
    summed_state = (inputs.astype(jnp.float32) + mixed_time).astype(jnp.bfloat16)
    upward = cotangent.reshape(clip_count, frames, 2, height, 2, breadth, 2, -1)
    upward = upward.transpose(0, 1, 3, 5, 2, 4, 6, 7).reshape(
        clip_count, frames, height, breadth, -1
    )
    flat_up = upward.reshape(-1, upward.shape[-1])
    state_grad = lax.dot_general(
        flat_up, up_weight, (((1,), (1,)), ((), ())), preferred_element_type=jnp.float32
    ).reshape(inputs.shape)
    up_grad = lax.dot_general(
        flat_up,
        summed_state.reshape(-1, channels),
        (((0,), (0,)), ((), ())),
        preferred_element_type=jnp.float32,
    )
    time_cot = state_grad.astype(jnp.bfloat16)
    flat_cot = time_cot.reshape(-1, channels)
    time_grad = jnp.stack(
        [
            lax.dot_general(
                flat_cot,
                act_window[:, 2 - time_tap : 2 - time_tap + frames].reshape(-1, channels),
                (((0,), (0,)), ((), ())),
                preferred_element_type=jnp.float32,
            )
            for time_tap in range(3)
        ]
    )
    following = from_behind(time_cot, TIME, -1)
    later_cot = jnp.concatenate((time_cot, following), axis=1)
    act_grad = along_time(later_cot, jnp.swapaxes(time_weight, 1, 2), frames, (0, 1, 2))
    sigmoid_part = jax.nn.sigmoid(normed)
    norm_grad = act_grad * sigmoid_part * (1.0 + normed * (1.0 - sigmoid_part))
    pre_grad = (
        (norm_grad - normed * jnp.mean(norm_grad * normed, -1, keepdims=True)) / rms_scale
    ).astype(jnp.bfloat16)
    grad_rimmed = with_halo(pre_grad, ((SPACE, 2),), 1)
    grad_window = jnp.pad(grad_rimmed, ((0, 0), (0, 0), (0, 0), (1, 1), (0, 0)))
    spatial_grad = filter_grad(input_rim, pre_grad, height, breadth)
    flipped = jnp.swapaxes(spatial_weight[::-1, ::-1], 2, 3)
    input_grad = (state_grad + spatial(grad_window, flipped, height, breadth)).astype(jnp.bfloat16)
    spatial_out, time_out, up_out = reduced(spatial_grad, time_grad, up_grad)
    return (input_grad, spatial_out, time_out, up_out)


def solution(mesh):
    whole = Mesh(
        mesh.devices.reshape(2, 4, 2, 2, 4, 4), ("y_lo", "x", "core", "y_hi", "z_hi", "z_lo")
    )
    tile = P("y_lo", TIME, SPACE, None, None)
    return jax.shard_map(
        local,
        mesh=whole,
        in_specs=(tile, tile, P(), P(), P()),
        out_specs=(
            tile,
            P(None, None, None, SPACE),
            P(None, None, SPACE),
            P(None, SPACE),
        ),
        check_vma=False,
    )
```

```python
import jax
import jax.numpy as jnp
from jax import lax
from jax.experimental import pallas as pl
from jax.experimental.pallas import tpu as pltpu
from jax.sharding import Mesh, PartitionSpec as P

epsilon = 1e-06
TIME = ("x", "core")
SPACE = ("y_hi", "z")
GROUP = ("y_lo", "x", "core")
PLANE = ("y_lo", "x", "core", "y_hi")
C = 256
W = 64
FRAMES = 2
ROWS = 2
PIX = FRAMES * ROWS * W
SPACES = 32
MEMBERS = 16
bf16 = jnp.bfloat16
f32 = jnp.float32


def dot(a, b):
    return lax.dot_general(a, b, (((1,), (0,)), ((), ())), preferred_element_type=f32)


def dot_bt(a, b):
    return lax.dot_general(a, b, (((1,), (1,)), ((), ())), preferred_element_type=f32)


def dot_at(a, b):
    return lax.dot_general(a, b, (((0,), (0,)), ((), ())), preferred_element_type=f32)


def column():
    return lax.broadcasted_iota(jnp.int32, (PIX, C), 0) & (W - 1)


def from_left(value):
    return jnp.where(column() == 0, 0.0, pltpu.roll(value, 1, 0))


def from_right(value):
    return jnp.where(column() == W - 1, 0.0, pltpu.roll(value, PIX - 1, 0))


def call(kernel, outs, flops, *operands):
    moved = sum(v.size * v.dtype.itemsize for v in operands)
    moved += sum(s.size * jnp.dtype(s.dtype).itemsize for s in outs)
    return pl.pallas_call(
        kernel,
        out_shape=outs,
        compiler_params=pltpu.CompilerParams(vmem_limit_bytes=40 << 20),
        cost_estimate=pl.CostEstimate(flops=flops, bytes_accessed=moved, transcendentals=0),
    )(*operands)


def shape(dims, dtype):
    return jax.ShapeDtypeStruct(dims, dtype)


def state_kernel(cot_ref, weight_ref, up_ref, state_ref, time_cot_ref):
    row = lax.broadcasted_iota(jnp.int32, (2 * W, 2 * W), 0)
    col = lax.broadcasted_iota(jnp.int32, (2 * W, 2 * W), 1)
    order = (col == 2 * (row & (W - 1)) + (row >> 6)).astype(f32).astype(bf16)
    for frame in range(FRAMES):
        for height in range(ROWS):
            first = (frame * ROWS + height) * W
            for t in range(2):
                pair = jnp.concatenate(
                    [cot_ref[2 * frame + t, 2 * height + p] for p in range(2)], axis=1
                )
                pair = dot(order, pair).astype(bf16)
                for p in range(2):
                    for q in range(2):
                        up_ref[2 * t + p, first : first + W, q * 128 : q * 128 + 128] = pair[
                            q * W : q * W + W, p * 128 : p * 128 + 128
                        ]
    state = None
    for at in range(4):
        part = dot_bt(up_ref[at], weight_ref[:, at * C : at * C + C])
        state = part if state is None else state + part
    state_ref[...] = state
    time_cot_ref[...] = state.astype(bf16)


def rows_at(block, low, high, offset):
    if offset == 0:
        return block[...].reshape(PIX, C)
    parts = []
    for frame in range(FRAMES):
        if offset < 0:
            parts += [low[frame], block[frame, 0]]
        else:
            parts += [block[frame, 1], high[frame]]
    return jnp.concatenate(parts, axis=0)


def forward_kernel(in_ref, low_ref, high_ref, weight_ref, normed_ref, scale_ref, act_ref):
    taps = [None] * 3
    for i in range(3):
        rows = rows_at(in_ref, low_ref, high_ref, i - 1)
        for j in range(3):
            part = dot(rows, weight_ref[i, j])
            taps[j] = part if taps[j] is None else taps[j] + part
    pre_act = from_left(taps[0]) + taps[1] + from_right(taps[2])
    scale = jnp.sqrt(jnp.mean(pre_act * pre_act, -1, keepdims=True) + epsilon)
    normed = pre_act / scale
    normed_ref[...] = normed
    scale_ref[...] = scale
    act_ref[...] = (normed / (1.0 + jnp.exp(-normed))).astype(bf16)


def pre_grad_kernel(cot_ref, later_ref, weight_ref, normed_ref, scale_ref, pre_ref):
    half = ROWS * W
    act_grad = dot_bt(cot_ref[...], weight_ref[0])
    middle = jnp.concatenate([cot_ref[half:, :], later_ref[:half, :]], axis=0)
    act_grad = act_grad + dot_bt(middle, weight_ref[1])
    act_grad = act_grad + dot_bt(later_ref[...], weight_ref[2])
    normed = normed_ref[...]
    sig = 1.0 / (1.0 + jnp.exp(-normed))
    norm_grad = act_grad * sig * (1.0 + normed * (1.0 - sig))
    mean = jnp.mean(norm_grad * normed, -1, keepdims=True)
    pre_ref[...] = ((norm_grad - normed * mean) / scale_ref[...]).astype(bf16)


def grads_kernel(
    in_ref, low_ref, high_ref, pre_ref, cot_ref, act_ref, earlier_ref, up_ref, weight_ref, out_ref
):
    half = ROWS * W
    pre = pre_ref[...]
    wide = pre.astype(f32)
    shifted = [from_right(wide).astype(bf16), pre, from_left(wide).astype(bf16)]
    acts = [
        act_ref[...],
        jnp.concatenate([earlier_ref[half:, :], act_ref[:half, :]], axis=0),
        earlier_ref[...],
    ]
    own = in_ref[...].reshape(PIX, C)
    mixed = dot(acts[0], weight_ref[0]) + dot(acts[1], weight_ref[1]) + dot(acts[2], weight_ref[2])
    state = (own.astype(f32) + mixed).astype(bf16)

    def tap(at):
        if at < 9:
            rows = rows_at(in_ref, low_ref, high_ref, at // 3 - 1)
            return dot_at(shifted[at % 3], rows).reshape(SPACES, 8, C)
        return dot_at(cot_ref[...], acts[at - 9]).reshape(SPACES, 8, C)

    for block in range(6):
        both = jnp.concatenate([tap(2 * block), tap(2 * block + 1)], axis=1).astype(bf16)
        out_ref[2 * block] = both[:, :, :128]
        out_ref[2 * block + 1] = both[:, :, 128:]
    for at in range(4):
        part = dot_at(up_ref[at], state).reshape(8, 32, C).astype(bf16)
        for low in range(2):
            for lane in range(2):
                out_ref[12 + 2 * low + lane, at * 8 : at * 8 + 8] = part[
                    :, low * 16 : low * 16 + 16, lane * 128 : lane * 128 + 128
                ]


def input_grad_kernel(state_ref, pre_ref, low_ref, high_ref, weight_ref, out_ref):
    taps = [None] * 3
    for i in range(3):
        rows = rows_at(pre_ref, low_ref, high_ref, 1 - i)
        for j in range(3):
            part = dot_bt(rows, weight_ref[i, j])
            taps[j] = part if taps[j] is None else taps[j] + part
    total = state_ref[...] + (from_right(taps[0]) + taps[1] + from_left(taps[2]))
    out_ref[...] = total.astype(bf16)


def unpack_kernel(in_ref, spatial_ref, time_ref, up_ref):
    for block in range(6):
        for lane in range(2):
            for low in range(2):
                at = 2 * block + low
                value = in_ref[2 * block + lane, low * 8 : low * 8 + 8, :]
                if at < 9:
                    spatial_ref[at, :, lane * 128 : lane * 128 + 128] = value
                else:
                    time_ref[at - 9, :, lane * 128 : lane * 128 + 128] = value
    for low in range(2):
        for lane in range(2):
            up_ref[low * 16 : low * 16 + 16, lane * 128 : lane * 128 + 128] = in_ref[
                12 + 2 * low + lane
            ]


def states(cotangent, up_weight):
    outs = (shape((4, PIX, C), bf16), shape((PIX, C), f32), shape((PIX, C), bf16))
    return call(state_kernel, outs, 10 * PIX * C * C, cotangent, up_weight)


def forward(inputs, low, high, weight):
    outs = (shape((PIX, C), f32), shape((PIX, 1), f32), shape((PIX, C), bf16))
    return call(forward_kernel, outs, 18 * PIX * C * C, inputs, low, high, weight)


def pre_gradient(time_cot, later, weight, normed, scale):
    outs = (shape((PIX, C), bf16),)
    return call(pre_grad_kernel, outs, 6 * PIX * C * C, time_cot, later, weight, normed, scale)[0]


def weight_grads(*operands):
    outs = (shape((MEMBERS, SPACES, 16, 128), bf16),)
    return call(grads_kernel, outs, 38 * PIX * C * C, *operands)[0]


def input_gradient(*operands):
    outs = (shape((PIX, C), bf16),)
    return call(input_grad_kernel, outs, 18 * PIX * C * C, *operands)[0]


def unpacked(gathered):
    outs = (shape((9, 8, C), f32), shape((3, 8, C), f32), shape((32, C), f32))
    return call(unpack_kernel, outs, 0, gathered)


def halo(block):
    forward_pairs = [(i, i + 1) for i in range(SPACES - 1)]
    backward_pairs = [(i + 1, i) for i in range(SPACES - 1)]
    low = lax.ppermute(block[:, ROWS - 1], SPACE, forward_pairs)
    high = lax.ppermute(block[:, 0], SPACE, backward_pairs)
    return low, high


def summed(parts):
    return jnp.sum(parts.astype(f32), axis=0)


def reduced(packed):
    value = packed.reshape(32, 16, 16, 128)
    value = summed(lax.all_to_all(value, PLANE, 0, 0)).astype(bf16)
    value = summed(lax.all_to_all(value, "z", 0, 0))
    value = jnp.broadcast_to(value[None], (MEMBERS, 16, 128))
    return unpacked(lax.all_to_all(value, GROUP, 0, 0))


def local(inputs, cotangent, spatial_weight, time_weight, up_weight):
    tile = inputs.reshape(FRAMES, ROWS, W, C)
    low, high = halo(tile)
    upward, state_grad, time_cot = states(cotangent.reshape(4, 4, 128, 128), up_weight)
    later = lax.ppermute(time_cot, TIME, [(i + 1, i) for i in range(7)])
    normed, scale, activated = forward(tile, low, high, spatial_weight)
    earlier = lax.ppermute(activated, TIME, [(i, i + 1) for i in range(7)])
    pre_grad = pre_gradient(time_cot, later, time_weight, normed, scale)
    packed = weight_grads(
        tile, low, high, pre_grad, time_cot, activated, earlier, upward, time_weight
    )
    pre_tile = pre_grad.reshape(FRAMES, ROWS, W, C)
    pre_low, pre_high = halo(pre_tile)
    spatial_grad, time_grad, up_grad = reduced(packed)
    input_grad = input_gradient(state_grad, pre_tile, pre_low, pre_high, spatial_weight)
    return (
        input_grad.reshape(inputs.shape),
        jnp.swapaxes(spatial_grad.reshape(3, 3, 8, C), 2, 3),
        jnp.swapaxes(time_grad, 1, 2),
        jnp.swapaxes(up_grad, 0, 1),
    )


def solution(mesh):
    whole = Mesh(mesh.devices.reshape(2, 4, 2, 2, 16), ("y_lo", "x", "core", "y_hi", "z"))
    tile = P("y_lo", TIME, SPACE, None, None)
    return jax.shard_map(
        local,
        mesh=whole,
        in_specs=(tile, tile, P(), P(), P()),
        out_specs=(tile, P(None, None, None, SPACE), P(None, None, SPACE), P(None, SPACE)),
        check_vma=False,
    )
```

```python
import jax
import jax.numpy as jnp
from jax import lax
from jax.experimental import pallas as pl
from jax.experimental.pallas import tpu as pltpu
from jax.sharding import Mesh, PartitionSpec as P

epsilon = 1e-06
TIME = ("x", "core")
SPACE = ("y_hi", "z")
GROUP = ("y_lo", "x", "core")
PLANE = ("y_lo", "x", "y_hi")
C = 256
W = 64
FRAMES = 2
ROWS = 2
PIX = FRAMES * ROWS * W
SPACES = 32
MEMBERS = 16
bf16 = jnp.bfloat16
f32 = jnp.float32


def dot(a, b):
    return lax.dot_general(a, b, (((1,), (0,)), ((), ())), preferred_element_type=f32)


def dot_bt(a, b):
    return lax.dot_general(a, b, (((1,), (1,)), ((), ())), preferred_element_type=f32)


def dot_at(a, b):
    return lax.dot_general(a, b, (((0,), (0,)), ((), ())), preferred_element_type=f32)


def column():
    return lax.broadcasted_iota(jnp.int32, (PIX, C), 0) & (W - 1)


def from_left(value):
    return jnp.where(column() == 0, 0.0, pltpu.roll(value, 1, 0))


def from_right(value):
    return jnp.where(column() == W - 1, 0.0, pltpu.roll(value, PIX - 1, 0))


def call(kernel, outs, flops, *operands, **given):
    moved = sum(v.size * v.dtype.itemsize for v in operands)
    moved += sum(s.size * jnp.dtype(s.dtype).itemsize for s in outs)
    return pl.pallas_call(
        kernel,
        out_shape=outs,
        compiler_params=pltpu.CompilerParams(vmem_limit_bytes=40 << 20),
        cost_estimate=pl.CostEstimate(flops=flops, bytes_accessed=moved, transcendentals=0),
        **given,
    )(*operands)


def shape(dims, dtype):
    return jax.ShapeDtypeStruct(dims, dtype)


def state_kernel(
    cot_hbm, up_weight_hbm, spatial_hbm, time_hbm, tile_hbm,
    up_ref, state_ref, time_cot_ref, spatial_ref, time_ref, tile_ref,
    cot_ref, weight_ref, sems,
):
    pairs = (
        (cot_hbm, cot_ref), (up_weight_hbm, weight_ref), (spatial_hbm, spatial_ref),
        (tile_hbm, tile_ref), (time_hbm, time_ref),
    )
    copies = [pltpu.make_async_copy(a, b, sems.at[at]) for at, (a, b) in enumerate(pairs)]
    for copy in copies:
        copy.start()
    row = lax.broadcasted_iota(jnp.int32, (2 * W, 2 * W), 0)
    col = lax.broadcasted_iota(jnp.int32, (2 * W, 2 * W), 1)
    order = (col == 2 * (row & (W - 1)) + (row >> 6)).astype(f32).astype(bf16)
    copies[0].wait()
    for frame in range(FRAMES):
        for height in range(ROWS):
            first = (frame * ROWS + height) * W
            for t in range(2):
                pair = jnp.concatenate(
                    [cot_ref[2 * frame + t, 2 * height + p] for p in range(2)], axis=1
                )
                pair = dot(order, pair).astype(bf16)
                for p in range(2):
                    for q in range(2):
                        up_ref[2 * t + p, first : first + W, q * 128 : q * 128 + 128] = pair[
                            q * W : q * W + W, p * 128 : p * 128 + 128
                        ]
    copies[1].wait()
    state = None
    for at in range(4):
        part = dot_bt(up_ref[at], weight_ref[:, at * C : at * C + C])
        state = part if state is None else state + part
    state_ref[...] = state
    time_cot_ref[...] = state.astype(bf16)
    for copy in copies[2:]:
        copy.wait()


def rows_at(block, low, high, offset):
    if offset == 0:
        return block[...].reshape(PIX, C)
    parts = []
    for frame in range(FRAMES):
        if offset < 0:
            parts += [low[frame], block[frame, 0]]
        else:
            parts += [block[frame, 1], high[frame]]
    return jnp.concatenate(parts, axis=0)


def forward_kernel(in_ref, low_ref, high_ref, weight_ref, normed_ref, scale_ref, act_ref):
    taps = [None] * 3
    for i in range(3):
        rows = rows_at(in_ref, low_ref, high_ref, i - 1)
        for j in range(3):
            part = dot(rows, weight_ref[i, j])
            taps[j] = part if taps[j] is None else taps[j] + part
    pre_act = from_left(taps[0]) + taps[1] + from_right(taps[2])
    scale = jnp.sqrt(jnp.mean(pre_act * pre_act, -1, keepdims=True) + epsilon)
    normed = pre_act / scale
    normed_ref[...] = normed
    scale_ref[...] = scale
    act_ref[...] = (normed / (1.0 + jnp.exp(-normed))).astype(bf16)


def pre_grad_kernel(cot_ref, later_ref, weight_ref, normed_ref, scale_ref, pre_ref):
    half = ROWS * W
    act_grad = dot_bt(cot_ref[...], weight_ref[0])
    middle = jnp.concatenate([cot_ref[half:, :], later_ref[:half, :]], axis=0)
    act_grad = act_grad + dot_bt(middle, weight_ref[1])
    act_grad = act_grad + dot_bt(later_ref[...], weight_ref[2])
    normed = normed_ref[...]
    sig = 1.0 / (1.0 + jnp.exp(-normed))
    norm_grad = act_grad * sig * (1.0 + normed * (1.0 - sig))
    mean = jnp.mean(norm_grad * normed, -1, keepdims=True)
    pre_ref[...] = ((norm_grad - normed * mean) / scale_ref[...]).astype(bf16)


def grads_kernel(
    core_ref, in_ref, low_ref, high_ref, pre_ref, cot_ref, act_ref, earlier_ref, up_ref, weight_ref,
    mine_ref, other_ref,
):
    half = ROWS * W
    first_core = core_ref[0] == 0

    def put(block, start, value):
        left, right = value[:, :, :128], value[:, :, 128:]
        count = value.shape[0]
        mine_ref[block, start : start + count] = jnp.where(first_core, left, right)
        other_ref[block, start : start + count] = jnp.where(first_core, right, left).astype(bf16)

    pre = pre_ref[...]
    wide = pre.astype(f32)
    shifted = [from_right(wide).astype(bf16), pre, from_left(wide).astype(bf16)]
    acts = [
        act_ref[...],
        jnp.concatenate([earlier_ref[half:, :], act_ref[:half, :]], axis=0),
        earlier_ref[...],
    ]
    own = in_ref[...].reshape(PIX, C)
    mixed = dot(acts[0], weight_ref[0]) + dot(acts[1], weight_ref[1]) + dot(acts[2], weight_ref[2])
    state = (own.astype(f32) + mixed).astype(bf16)

    def tap(at):
        if at < 9:
            rows = rows_at(in_ref, low_ref, high_ref, at // 3 - 1)
            return dot_at(shifted[at % 3], rows).reshape(SPACES, 8, C)
        return dot_at(cot_ref[...], acts[at - 9]).reshape(SPACES, 8, C)

    for block in range(6):
        put(block, 0, jnp.concatenate([tap(2 * block), tap(2 * block + 1)], axis=1))
    for at in range(4):
        part = dot_at(up_ref[at], state).reshape(8, 32, C)
        for low in range(2):
            put(6 + low, at * 8, part[:, low * 16 : low * 16 + 16])


def swap_sum_kernel(mine_ref, arrived_ref, out_ref):
    for block in range(8):
        out_ref[block] = (mine_ref[block] + arrived_ref[block].astype(f32)).astype(bf16)


def plane_sum_kernel(parts_ref, out_ref):
    total = parts_ref[0].astype(f32)
    for at in range(1, 16):
        total = total + parts_ref[at].astype(f32)
    out_ref[...] = total.astype(bf16)


def depth_sum_kernel(parts_ref, out_ref):
    total = parts_ref[0].astype(f32)
    for at in range(1, 16):
        total = total + parts_ref[at].astype(f32)
    for at in range(MEMBERS):
        out_ref[at] = total


def input_grad_kernel(state_ref, pre_ref, low_ref, high_ref, weight_ref, out_ref):
    taps = [None] * 3
    for i in range(3):
        rows = rows_at(pre_ref, low_ref, high_ref, 1 - i)
        for j in range(3):
            part = dot_bt(rows, weight_ref[i, j])
            taps[j] = part if taps[j] is None else taps[j] + part
    total = state_ref[...] + (from_right(taps[0]) + taps[1] + from_left(taps[2]))
    out_ref[...] = total.astype(bf16)


def unpack_kernel(in_ref, spatial_ref, time_ref, up_ref):
    for block in range(6):
        for lane in range(2):
            for low in range(2):
                at = 2 * block + low
                value = in_ref[2 * block + lane, low * 8 : low * 8 + 8, :]
                if at < 9:
                    spatial_ref[at, :, lane * 128 : lane * 128 + 128] = value
                else:
                    time_ref[at - 9, :, lane * 128 : lane * 128 + 128] = value
    for low in range(2):
        for lane in range(2):
            up_ref[low * 16 : low * 16 + 16, lane * 128 : lane * 128 + 128] = in_ref[
                12 + 2 * low + lane
            ]


def states(cotangent, up_weight, spatial_weight, time_weight, tile):
    outs = (
        shape((4, PIX, C), bf16), shape((PIX, C), f32), shape((PIX, C), bf16),
        shape(spatial_weight.shape, bf16), shape(time_weight.shape, bf16), shape(tile.shape, bf16),
    )
    return call(
        state_kernel,
        outs,
        10 * PIX * C * C,
        cotangent, up_weight, spatial_weight, time_weight, tile,
        in_specs=[pl.BlockSpec(memory_space=pltpu.HBM)] * 5,
        scratch_shapes=[
            pltpu.VMEM(cotangent.shape, bf16),
            pltpu.VMEM(up_weight.shape, bf16),
            pltpu.SemaphoreType.DMA((5,)),
        ],
    )


def forward(inputs, low, high, weight):
    outs = (shape((PIX, C), f32), shape((PIX, 1), f32), shape((PIX, C), bf16))
    return call(forward_kernel, outs, 18 * PIX * C * C, inputs, low, high, weight)


def pre_gradient(time_cot, later, weight, normed, scale):
    outs = (shape((PIX, C), bf16),)
    return call(pre_grad_kernel, outs, 6 * PIX * C * C, time_cot, later, weight, normed, scale)[0]


def weight_grads(*operands):
    outs = (shape((8, SPACES, 16, 128), f32), shape((8, SPACES, 16, 128), bf16))
    specs = [pl.BlockSpec(memory_space=pltpu.SMEM)]
    specs += [pl.BlockSpec(memory_space=pltpu.VMEM)] * (len(operands) - 1)
    return call(grads_kernel, outs, 38 * PIX * C * C, *operands, in_specs=specs)


def input_gradient(*operands):
    outs = (shape((PIX, C), bf16),)
    return call(input_grad_kernel, outs, 18 * PIX * C * C, *operands)[0]


def unpacked(gathered):
    outs = (shape((9, 8, C), f32), shape((3, 8, C), f32), shape((32, C), f32))
    return call(unpack_kernel, outs, 0, gathered)


def halo(block):
    forward_pairs = [(i, i + 1) for i in range(SPACES - 1)]
    backward_pairs = [(i + 1, i) for i in range(SPACES - 1)]
    low = lax.ppermute(block[:, ROWS - 1], SPACE, forward_pairs)
    high = lax.ppermute(block[:, 0], SPACE, backward_pairs)
    return low, high


def local(inputs, cotangent, spatial_weight, time_weight, up_weight):
    tile = inputs.reshape(FRAMES, ROWS, W, C)
    low, high = halo(tile)
    upward, state_grad, time_cot, spatial_weight, time_weight, tile = states(
        cotangent.reshape(4, 4, 128, 128), up_weight, spatial_weight, time_weight, tile
    )
    later = lax.ppermute(time_cot, TIME, [(i + 1, i) for i in range(7)])
    normed, scale, activated = forward(tile, low, high, spatial_weight)
    earlier = lax.ppermute(activated, TIME, [(i, i + 1) for i in range(7)])
    pre_grad = pre_gradient(time_cot, later, time_weight, normed, scale)
    core = lax.axis_index("core").astype(jnp.int32).reshape(1)
    mine, other = weight_grads(
        core, tile, low, high, pre_grad, time_cot, activated, earlier, upward, time_weight
    )
    other = lax.ppermute(other, "core", [(0, 1), (1, 0)])
    value = call(swap_sum_kernel, (shape(mine.shape, bf16),), 0, mine, other)[0]
    pre_tile = pre_grad.reshape(FRAMES, ROWS, W, C)
    edges, value = lax.optimization_barrier((pre_tile, value))
    value = lax.all_to_all(value.reshape(16, 16, 16, 128), PLANE, 0, 0)
    pre_low, pre_high = halo(edges)
    input_grad = input_gradient(state_grad, pre_tile, pre_low, pre_high, spatial_weight)
    value, input_grad = lax.optimization_barrier((value, input_grad))
    value = call(plane_sum_kernel, (shape((16, 16, 128), bf16),), 0, value)[0]
    value = lax.all_to_all(value, "z", 0, 0)
    value = call(depth_sum_kernel, (shape((MEMBERS, 16, 128), f32),), 0, value)[0]
    spatial_grad, time_grad, up_grad = unpacked(lax.all_to_all(value, GROUP, 0, 0))
    return (
        input_grad.reshape(inputs.shape),
        jnp.swapaxes(spatial_grad.reshape(3, 3, 8, C), 2, 3),
        jnp.swapaxes(time_grad, 1, 2),
        jnp.swapaxes(up_grad, 0, 1),
    )


def solution(mesh):
    whole = Mesh(mesh.devices.reshape(2, 4, 2, 2, 16), ("y_lo", "x", "core", "y_hi", "z"))
    tile = P("y_lo", TIME, SPACE, None, None)
    return jax.shard_map(
        local,
        mesh=whole,
        in_specs=(tile, tile, P(), P(), P()),
        out_specs=(tile, P(None, None, None, SPACE), P(None, None, SPACE), P(None, SPACE)),
        check_vma=False,
    )
```

```python
import jax
import jax.numpy as jnp
from jax import lax
from jax.experimental import pallas as pl
from jax.experimental.pallas import tpu as pltpu
from jax.sharding import Mesh, PartitionSpec as P

epsilon = 1e-06
TIME = ("x", "core")
SPACE = ("y_hi", "z")
GROUP = ("y_lo", "x", "core")
PLANE = ("y_lo", "x", "y_hi")
C = 256
W = 64
FRAMES = 2
ROWS = 2
PIX = FRAMES * ROWS * W
SPACES = 32
MEMBERS = 16
bf16 = jnp.bfloat16
f32 = jnp.float32


def dot(a, b):
    return lax.dot_general(a, b, (((1,), (0,)), ((), ())), preferred_element_type=f32)


def dot_bt(a, b):
    return lax.dot_general(a, b, (((1,), (1,)), ((), ())), preferred_element_type=f32)


def dot_at(a, b):
    return lax.dot_general(a, b, (((0,), (0,)), ((), ())), preferred_element_type=f32)


def column():
    return lax.broadcasted_iota(jnp.int32, (PIX, C), 0) & (W - 1)


def from_left(value):
    return jnp.where(column() == 0, 0.0, pltpu.roll(value, 1, 0))


def from_right(value):
    return jnp.where(column() == W - 1, 0.0, pltpu.roll(value, PIX - 1, 0))


def call(kernel, outs, flops, *operands, **given):
    moved = sum(v.size * v.dtype.itemsize for v in operands)
    moved += sum(s.size * jnp.dtype(s.dtype).itemsize for s in outs)
    return pl.pallas_call(
        kernel,
        out_shape=outs,
        compiler_params=pltpu.CompilerParams(vmem_limit_bytes=40 << 20),
        cost_estimate=pl.CostEstimate(flops=flops, bytes_accessed=moved, transcendentals=0),
        **given,
    )(*operands)


def shape(dims, dtype):
    return jax.ShapeDtypeStruct(dims, dtype)


def arranged(cot_ref, up_ref):
    row = lax.broadcasted_iota(jnp.int32, (2 * W, 2 * W), 0)
    col = lax.broadcasted_iota(jnp.int32, (2 * W, 2 * W), 1)
    order = (col == 2 * (row & (W - 1)) + (row >> 6)).astype(f32).astype(bf16)
    for frame in range(FRAMES):
        for height in range(ROWS):
            first = (frame * ROWS + height) * W
            for t in range(2):
                pair = jnp.concatenate(
                    [cot_ref[2 * frame + t, 2 * height + p] for p in range(2)], axis=1
                )
                pair = dot(order, pair).astype(bf16)
                for p in range(2):
                    for q in range(2):
                        up_ref[2 * t + p, first : first + W, q * 128 : q * 128 + 128] = pair[
                            q * W : q * W + W, p * 128 : p * 128 + 128
                        ]


def state_of(up_ref, weight_ref):
    state = None
    for at in range(4):
        part = dot_bt(up_ref[at], weight_ref[:, at * C : at * C + C])
        state = part if state is None else state + part
    return state


def state_kernel(cot_ref, weight_ref, up_ref, state_ref, time_cot_ref):
    arranged(cot_ref, up_ref)
    state = state_of(up_ref, weight_ref)
    state_ref[...] = state
    time_cot_ref[...] = state.astype(bf16)


def rows_at(block, low, high, offset):
    if offset == 0:
        return block[...].reshape(PIX, C)
    parts = []
    for frame in range(FRAMES):
        if offset < 0:
            parts += [low[frame], block[frame, 0]]
        else:
            parts += [block[frame, 1], high[frame]]
    return jnp.concatenate(parts, axis=0)


def forward_kernel(in_ref, low_ref, high_ref, weight_ref, normed_ref, scale_ref, act_ref):
    taps = [None] * 3
    for i in range(3):
        rows = rows_at(in_ref, low_ref, high_ref, i - 1)
        for j in range(3):
            part = dot(rows, weight_ref[i, j])
            taps[j] = part if taps[j] is None else taps[j] + part
    pre_act = from_left(taps[0]) + taps[1] + from_right(taps[2])
    scale = jnp.sqrt(jnp.mean(pre_act * pre_act, -1, keepdims=True) + epsilon)
    normed = pre_act / scale
    normed_ref[...] = normed
    scale_ref[...] = scale
    act_ref[...] = (normed / (1.0 + jnp.exp(-normed))).astype(bf16)


def grads_kernel(
    core_ref, in_ref, low_ref, high_ref, normed_ref, scale_ref, act_ref, cot_ref, up_ref, later_ref,
    time_ref, weight_ref, pre_ref, mine_ref, other_ref, later_up_ref,
):
    half = ROWS * W
    first_core = core_ref[0] == 0

    def put(block, start, value):
        value = value.astype(bf16)
        left, right = value[:, :, :128], value[:, :, 128:]
        count = value.shape[0]
        mine_ref[block, start : start + count] = jnp.where(first_core, left, right)
        other_ref[block, start : start + count] = jnp.where(first_core, right, left)

    arranged(later_ref, later_up_ref)
    later_cot = state_of(later_up_ref, weight_ref).astype(bf16)
    cots = [
        cot_ref[...],
        jnp.concatenate([cot_ref[half:, :], later_cot[:half, :]], axis=0),
        later_cot,
    ]
    act_grad = dot_bt(cots[0], time_ref[0]) + dot_bt(cots[1], time_ref[1])
    act_grad = act_grad + dot_bt(cots[2], time_ref[2])
    normed = normed_ref[...]
    sig = 1.0 / (1.0 + jnp.exp(-normed))
    norm_grad = act_grad * sig * (1.0 + normed * (1.0 - sig))
    mean = jnp.mean(norm_grad * normed, -1, keepdims=True)
    pre = ((norm_grad - normed * mean) / scale_ref[...]).astype(bf16)
    pre_ref[...] = pre
    wide = pre.astype(f32)
    shifted = [from_right(wide).astype(bf16), pre, from_left(wide).astype(bf16)]
    act = act_ref[...]
    own = in_ref[...].reshape(PIX, C)
    mixed = [
        (own.astype(f32) + dot(act, time_ref[0])).astype(bf16),
        dot(act, time_ref[1]).astype(bf16),
        dot(act, time_ref[2]).astype(bf16),
    ]

    def tap(at):
        if at < 9:
            rows = rows_at(in_ref, low_ref, high_ref, at // 3 - 1)
            return dot_at(shifted[at % 3], rows).reshape(SPACES, 8, C)
        return dot_at(cots[at - 9], act).reshape(SPACES, 8, C)

    for block in range(6):
        put(block, 0, jnp.concatenate([tap(2 * block), tap(2 * block + 1)], axis=1))
    for at in range(4):
        part = dot_at(up_ref[at], mixed[0])
        part = part + dot_at(up_ref[at, half:, :], mixed[1][:half, :])
        part = part + dot_at(later_up_ref[at, :half, :], mixed[1][half:, :])
        part = part + dot_at(later_up_ref[at], mixed[2])
        part = part.reshape(8, 32, C)
        for low in range(2):
            put(6 + low, at * 8, part[:, low * 16 : low * 16 + 16])


def swap_sum_kernel(mine_ref, arrived_ref, out_ref):
    for block in range(8):
        total = mine_ref[block].astype(f32) + arrived_ref[block].astype(f32)
        out_ref[block] = total.astype(bf16)


def plane_sum_kernel(parts_ref, out_ref):
    total = parts_ref[0].astype(f32)
    for at in range(1, 16):
        total = total + parts_ref[at].astype(f32)
    out_ref[...] = total.astype(bf16)


def depth_sum_kernel(parts_ref, out_ref):
    total = parts_ref[0].astype(f32)
    for at in range(1, 16):
        total = total + parts_ref[at].astype(f32)
    for at in range(MEMBERS):
        out_ref[at] = total


def input_grad_kernel(state_ref, pre_ref, low_ref, high_ref, weight_ref, out_ref):
    taps = [None] * 3
    for i in range(3):
        rows = rows_at(pre_ref, low_ref, high_ref, 1 - i)
        for j in range(3):
            part = dot_bt(rows, weight_ref[i, j])
            taps[j] = part if taps[j] is None else taps[j] + part
    total = state_ref[...] + (from_right(taps[0]) + taps[1] + from_left(taps[2]))
    out_ref[...] = total.astype(bf16)


def unpack_kernel(in_ref, spatial_ref, time_ref, up_ref):
    for block in range(6):
        for lane in range(2):
            for low in range(2):
                at = 2 * block + low
                value = in_ref[2 * block + lane, low * 8 : low * 8 + 8, :]
                if at < 9:
                    spatial_ref[at, :, lane * 128 : lane * 128 + 128] = value
                else:
                    time_ref[at - 9, :, lane * 128 : lane * 128 + 128] = value
    for low in range(2):
        for lane in range(2):
            up_ref[low * 16 : low * 16 + 16, lane * 128 : lane * 128 + 128] = in_ref[
                12 + 2 * low + lane
            ]


def states(cotangent, up_weight):
    outs = (shape((4, PIX, C), bf16), shape((PIX, C), f32), shape((PIX, C), bf16))
    return call(state_kernel, outs, 10 * PIX * C * C, cotangent, up_weight)


def forward(inputs, low, high, weight):
    outs = (shape((PIX, C), f32), shape((PIX, 1), f32), shape((PIX, C), bf16))
    return call(forward_kernel, outs, 18 * PIX * C * C, inputs, low, high, weight)


def gradients(*operands):
    half = shape((8, SPACES, 16, 128), bf16)
    specs = [pl.BlockSpec(memory_space=pltpu.SMEM)]
    specs += [pl.BlockSpec(memory_space=pltpu.VMEM)] * (len(operands) - 1)
    return call(
        grads_kernel,
        (shape((PIX, C), bf16), half, half),
        68 * PIX * C * C,
        *operands,
        in_specs=specs,
        scratch_shapes=[pltpu.VMEM((4, PIX, C), bf16)],
    )


def input_gradient(*operands):
    outs = (shape((PIX, C), bf16),)
    return call(input_grad_kernel, outs, 18 * PIX * C * C, *operands)[0]


def unpacked(gathered):
    outs = (shape((9, 8, C), f32), shape((3, 8, C), f32), shape((32, C), f32))
    return call(unpack_kernel, outs, 0, gathered)


def halo(block):
    even = (lax.axis_index(SPACE) & 1) == 0
    top, bottom = block[:, 0], block[:, ROWS - 1]
    pairs = [[(i, i + 1) for i in range(start, SPACES - 1, 2)] for start in (0, 1)]
    pairs = [found + [(b, a) for a, b in found] for found in pairs]
    first = lax.ppermute(jnp.where(even, bottom, top), SPACE, pairs[0])
    second = lax.ppermute(jnp.where(even, top, bottom), SPACE, pairs[1])
    return jnp.where(even, second, first), jnp.where(even, first, second)


def local(inputs, cotangent, spatial_weight, time_weight, up_weight):
    tile = inputs.reshape(FRAMES, ROWS, W, C)
    cotangent = cotangent.reshape(2 * FRAMES, 2 * ROWS, 2 * W, -1)
    later = lax.ppermute(cotangent, TIME, [(i + 1, i) for i in range(7)])
    low, high = halo(tile)
    upward, state_grad, time_cot = states(cotangent, up_weight)
    normed, scale, activated = forward(tile, low, high, spatial_weight)
    core = lax.axis_index("core").astype(jnp.int32).reshape(1)
    pre_grad, mine, other = gradients(
        core, tile, low, high, normed, scale, activated, time_cot, upward, later,
        time_weight, up_weight,
    )
    other = lax.ppermute(other, "core", [(0, 1), (1, 0)])
    value = call(swap_sum_kernel, (shape(mine.shape, bf16),), 0, mine, other)[0]
    pre_tile = pre_grad.reshape(FRAMES, ROWS, W, C)
    edges, value = lax.optimization_barrier((pre_tile, value))
    value = lax.all_to_all(value.reshape(16, 16, 16, 128), PLANE, 0, 0)
    pre_low, pre_high = halo(edges)
    input_grad = input_gradient(state_grad, pre_tile, pre_low, pre_high, spatial_weight)
    value, input_grad = lax.optimization_barrier((value, input_grad))
    value = call(plane_sum_kernel, (shape((16, 16, 128), bf16),), 0, value)[0]
    value = lax.all_to_all(value, "z", 0, 0)
    value = call(depth_sum_kernel, (shape((MEMBERS, 16, 128), f32),), 0, value)[0]
    spatial_grad, time_grad, up_grad = unpacked(lax.all_to_all(value, GROUP, 0, 0))
    return (
        input_grad.reshape(inputs.shape),
        jnp.swapaxes(spatial_grad.reshape(3, 3, 8, C), 2, 3),
        jnp.swapaxes(time_grad, 1, 2),
        jnp.swapaxes(up_grad, 0, 1),
    )


def solution(mesh):
    whole = Mesh(mesh.devices.reshape(2, 4, 2, 2, 16), ("y_lo", "x", "core", "y_hi", "z"))
    tile = P("y_lo", TIME, SPACE, None, None)
    return jax.shard_map(
        local,
        mesh=whole,
        in_specs=(tile, tile, P(), P(), P()),
        out_specs=(tile, P(None, None, None, SPACE), P(None, None, SPACE), P(None, SPACE)),
        check_vma=False,
    )
```

```python
import jax
import jax.numpy as jnp
from jax import lax
from jax.experimental import pallas as pl
from jax.experimental.pallas import tpu as pltpu
from jax.sharding import Mesh, PartitionSpec as P

epsilon = 1e-06
TIME = ("x", "core")
SPACE = ("y_hi", "z")
GROUP = ("y_lo", "x", "core")
PLANE = ("y_lo", "x", "y_hi")
C = 256
W = 64
FRAMES = 2
ROWS = 2
PIX = FRAMES * ROWS * W
SPACES = 32
MEMBERS = 16
ROOM = 62
bf16 = jnp.bfloat16
f32 = jnp.float32


def dot(a, b):
    return lax.dot_general(a, b, (((1,), (0,)), ((), ())), preferred_element_type=f32)


def dot_bt(a, b):
    return lax.dot_general(a, b, (((1,), (1,)), ((), ())), preferred_element_type=f32)


def dot_at(a, b):
    return lax.dot_general(a, b, (((0,), (0,)), ((), ())), preferred_element_type=f32)


def column():
    return lax.broadcasted_iota(jnp.int32, (PIX, C), 0) & (W - 1)


def from_left(value):
    return jnp.where(column() == 0, 0.0, pltpu.roll(value, 1, 0))


def from_right(value):
    return jnp.where(column() == W - 1, 0.0, pltpu.roll(value, PIX - 1, 0))


def call(kernel, outs, flops, *operands, room=40, **given):
    moved = sum(v.size * v.dtype.itemsize for v in operands)
    moved += sum(s.size * s.dtype.itemsize for s in jax.tree.leaves(outs))
    return pl.pallas_call(
        kernel,
        out_shape=outs,
        compiler_params=pltpu.CompilerParams(vmem_limit_bytes=room << 20),
        cost_estimate=pl.CostEstimate(flops=flops, bytes_accessed=moved, transcendentals=0),
        **given,
    )(*operands)


def with_scalars(operands):
    specs = [pl.BlockSpec(memory_space=pltpu.SMEM)]
    return specs + [pl.BlockSpec(memory_space=pltpu.VMEM)] * (len(operands) - 1)


def shape(dims, dtype):
    return jax.ShapeDtypeStruct(dims, dtype)


def arranged(cot_ref, up_ref):
    row = lax.broadcasted_iota(jnp.int32, (2 * W, 2 * W), 0)
    col = lax.broadcasted_iota(jnp.int32, (2 * W, 2 * W), 1)
    order = (col == 2 * (row & (W - 1)) + (row >> 6)).astype(f32).astype(bf16)
    for frame in range(FRAMES):
        for height in range(ROWS):
            first = (frame * ROWS + height) * W
            for t in range(2):
                pair = jnp.concatenate(
                    [cot_ref[2 * frame + t, 2 * height + p] for p in range(2)], axis=1
                )
                pair = dot(order, pair).astype(bf16)
                for p in range(2):
                    for q in range(2):
                        up_ref[2 * t + p, first : first + W, q * 128 : q * 128 + 128] = pair[
                            q * W : q * W + W, p * 128 : p * 128 + 128
                        ]


def state_of(up_ref, weight_ref):
    state = None
    for at in range(4):
        part = dot_bt(up_ref[at], weight_ref[:, at * C : at * C + C])
        state = part if state is None else state + part
    return state


def state_kernel(
    cot_ref, later_ref, weight_ref, up_ref, later_up_ref, state_ref, time_cot_ref, later_cot_ref
):
    arranged(cot_ref, up_ref)
    state = state_of(up_ref, weight_ref)
    state_ref[...] = state
    time_cot_ref[...] = state.astype(bf16)
    arranged(later_ref, later_up_ref)
    later_cot_ref[...] = state_of(later_up_ref, weight_ref).astype(bf16)


def rows_at(block, low, high, offset):
    if offset == 0:
        return block[...].reshape(PIX, C)
    parts = []
    for frame in range(FRAMES):
        if offset < 0:
            parts += [low[frame], block[frame, 0]]
        else:
            parts += [block[frame, 1], high[frame]]
    return jnp.concatenate(parts, axis=0)


def sides(where_ref, first_ref, second_ref):
    even = where_ref[1] == 0
    first, second = first_ref[...], second_ref[...]
    return jnp.where(even, second, first), jnp.where(even, first, second)


def edge_kernel(where_ref, tile_ref, first_ref, second_ref, sems):
    odd = where_ref[1]
    copies = []
    for frame in range(FRAMES):
        for at, (row, out) in enumerate(((1 - odd, first_ref), (odd, second_ref))):
            copies.append(
                pltpu.make_async_copy(
                    tile_ref.at[frame, row], out.at[frame], sems.at[2 * frame + at]
                )
            )
    for copy in copies:
        copy.start()
    for copy in copies:
        copy.wait()


def grads_kernel(
    where_ref, in_ref, first_ref, second_ref, spatial_ref, cot_ref, later_cot, up_ref,
    later_up_ref, time_ref, pre_ref, mine_ref, other_ref,
):
    half = ROWS * W
    first_core = where_ref[0] == 0
    low, high = sides(where_ref, first_ref, second_ref)

    def put(block, start, value):
        value = value.astype(bf16)
        left, right = value[:, :, :128], value[:, :, 128:]
        count = value.shape[0]
        mine_ref[block, start : start + count] = jnp.where(first_core, left, right)
        other_ref[block, start : start + count] = jnp.where(first_core, right, left)

    taps = [None] * 3
    for i in range(3):
        rows = rows_at(in_ref, low, high, i - 1)
        for j in range(3):
            part = dot(rows, spatial_ref[i, j])
            taps[j] = part if taps[j] is None else taps[j] + part
    pre_act = from_left(taps[0]) + taps[1] + from_right(taps[2])
    scale = jnp.sqrt(jnp.mean(pre_act * pre_act, -1, keepdims=True) + epsilon)
    normed = pre_act / scale
    sig = 1.0 / (1.0 + jnp.exp(-normed))
    act = (normed / (1.0 + jnp.exp(-normed))).astype(bf16)
    cots = [
        cot_ref[...],
        jnp.concatenate([cot_ref[half:, :], later_cot[:half, :]], axis=0),
        later_cot[...],
    ]
    act_grad = dot_bt(cots[0], time_ref[0]) + dot_bt(cots[1], time_ref[1])
    act_grad = act_grad + dot_bt(cots[2], time_ref[2])
    norm_grad = act_grad * sig * (1.0 + normed * (1.0 - sig))
    mean = jnp.mean(norm_grad * normed, -1, keepdims=True)
    pre = ((norm_grad - normed * mean) / scale).astype(bf16)
    pre_ref[...] = pre
    wide = pre.astype(f32)
    shifted = [from_right(wide).astype(bf16), pre, from_left(wide).astype(bf16)]
    own = in_ref[...].reshape(PIX, C)
    mixed = [
        (own.astype(f32) + dot(act, time_ref[0])).astype(bf16),
        dot(act, time_ref[1]).astype(bf16),
        dot(act, time_ref[2]).astype(bf16),
    ]

    def tap(at):
        if at < 9:
            rows = rows_at(in_ref, low, high, at // 3 - 1)
            return dot_at(shifted[at % 3], rows).reshape(SPACES, 8, C)
        return dot_at(cots[at - 9], act).reshape(SPACES, 8, C)

    for block in range(6):
        put(block, 0, jnp.concatenate([tap(2 * block), tap(2 * block + 1)], axis=1))
    for at in range(4):
        part = dot_at(up_ref[at], mixed[0])
        part = part + dot_at(up_ref[at, half:, :], mixed[1][:half, :])
        part = part + dot_at(later_up_ref[at, :half, :], mixed[1][half:, :])
        part = part + dot_at(later_up_ref[at], mixed[2])
        part = part.reshape(8, 32, C)
        for low in range(2):
            put(6 + low, at * 8, part[:, low * 16 : low * 16 + 16])


def swap_sum_kernel(mine_ref, arrived_ref, out_ref):
    out_ref[...] = (mine_ref[...].astype(f32) + arrived_ref[...].astype(f32)).astype(bf16)


def plane_sum_kernel(parts_ref, out_ref):
    total = parts_ref[0].astype(f32)
    for at in range(1, 16):
        total = total + parts_ref[at].astype(f32)
    out_ref[...] = total


def input_grad_kernel(
    where_ref, state_ref, pre_ref, first_ref, second_ref, weight_ref, out_ref
):
    low, high = sides(where_ref, first_ref, second_ref)
    taps = [None] * 3
    for i in range(3):
        rows = rows_at(pre_ref, low, high, 1 - i)
        for j in range(3):
            part = dot_bt(rows, weight_ref[i, j])
            taps[j] = part if taps[j] is None else taps[j] + part
    total = state_ref[...] + (from_right(taps[0]) + taps[1] + from_left(taps[2]))
    out_ref[...] = total.astype(bf16)


def unpack_kernel(in_ref, spatial_ref, time_ref, up_ref):
    for block in range(6):
        for lane in range(2):
            for low in range(2):
                at = 2 * block + low
                value = in_ref[2 * block + lane, low * 8 : low * 8 + 8, :]
                if at < 9:
                    spatial_ref[at, :, lane * 128 : lane * 128 + 128] = value
                else:
                    time_ref[at - 9, :, lane * 128 : lane * 128 + 128] = value
    for low in range(2):
        for lane in range(2):
            up_ref[low * 16 : low * 16 + 16, lane * 128 : lane * 128 + 128] = in_ref[
                12 + 2 * low + lane
            ]


def edges(where, tile):
    row = shape((FRAMES, W, C), bf16)
    return call(
        edge_kernel,
        (row, row),
        0,
        where,
        tile,
        room=ROOM,
        in_specs=[pl.BlockSpec(memory_space=pltpu.SMEM), pl.BlockSpec(memory_space=pltpu.HBM)],
        scratch_shapes=[pltpu.SemaphoreType.DMA((4,))],
    )


def states(cotangent, later, up_weight):
    up = shape((4, PIX, C), bf16)
    flat = shape((PIX, C), bf16)
    outs = (up, up, shape((PIX, C), f32), flat, flat)
    return call(state_kernel, outs, 20 * PIX * C * C, cotangent, later, up_weight)


def gradients(*operands):
    half = shape((8, SPACES, 16, 128), bf16)
    outs = (shape((PIX, C), bf16), half, half)
    specs = with_scalars(operands)
    return call(grads_kernel, outs, 76 * PIX * C * C, *operands, in_specs=specs)


def swap_sum(mine, arrived):
    block = pl.BlockSpec((1, SPACES, 16, 128), lambda at: (at, 0, 0, 0))
    return call(
        swap_sum_kernel,
        shape(mine.shape, bf16),
        0,
        mine,
        arrived,
        grid=(8,),
        in_specs=[block, block],
        out_specs=block,
    )


def input_gradient(*operands):
    outs = (shape((PIX, C), bf16),)
    specs = with_scalars(operands)
    return call(input_grad_kernel, outs, 18 * PIX * C * C, *operands, in_specs=specs)[0]


def unpacked(gathered):
    outs = (shape((9, 8, C), f32), shape((3, 8, C), f32), shape((32, C), f32))
    return call(unpack_kernel, outs, 0, gathered)


def halo(first, second):
    pairs = [[(i, i + 1) for i in range(start, SPACES - 1, 2)] for start in (0, 1)]
    pairs = [found + [(b, a) for a, b in found] for found in pairs]
    return lax.ppermute(first, SPACE, pairs[0]), lax.ppermute(second, SPACE, pairs[1])


def local(inputs, cotangent, spatial_weight, time_weight, up_weight):
    odd = lax.axis_index("z") & 1
    where = jnp.stack([lax.axis_index("core"), odd]).astype(jnp.int32)
    tile = inputs.reshape(FRAMES, ROWS, W, C)
    cotangent = cotangent.reshape(2 * FRAMES, 2 * ROWS, 2 * W, -1)
    later = lax.ppermute(cotangent, TIME, [(i + 1, i) for i in range(7)])
    first, second = halo(*edges(where, tile))
    upward, later_up, state_grad, time_cot, later_cot = states(cotangent, later, up_weight)
    pre_grad, mine, other = gradients(
        where, tile, first, second, spatial_weight, time_cot, later_cot, upward, later_up,
        time_weight,
    )
    other = lax.ppermute(other, "core", [(0, 1), (1, 0)])
    value = swap_sum(mine, other)
    pre_tile = pre_grad.reshape(FRAMES, ROWS, W, C)
    held, value = lax.optimization_barrier((pre_tile, value))
    value = lax.all_to_all(value.reshape(16, 16, 16, 128), PLANE, 0, 0)
    top, bottom = held[:, 0], held[:, ROWS - 1]
    even = odd == 0
    first, second = halo(jnp.where(even, bottom, top), jnp.where(even, top, bottom))
    input_grad = input_gradient(where, state_grad, pre_tile, first, second, spatial_weight)
    value, input_grad = lax.optimization_barrier((value, input_grad))
    value = call(plane_sum_kernel, (shape((16, 16, 128), f32),), 0, value)[0]
    value = lax.psum_scatter(value, "z", scatter_dimension=0)
    value = jnp.broadcast_to(value[None], (MEMBERS, 16, 128))
    spatial_grad, time_grad, up_grad = unpacked(lax.all_to_all(value, GROUP, 0, 0))
    return (
        input_grad.reshape(inputs.shape),
        jnp.swapaxes(spatial_grad.reshape(3, 3, 8, C), 2, 3),
        jnp.swapaxes(time_grad, 1, 2),
        jnp.swapaxes(up_grad, 0, 1),
    )


def solution(mesh):
    whole = Mesh(mesh.devices.reshape(2, 4, 2, 2, 16), ("y_lo", "x", "core", "y_hi", "z"))
    tile = P("y_lo", TIME, SPACE, None, None)
    return jax.shard_map(
        local,
        mesh=whole,
        in_specs=(tile, tile, P(), P(), P()),
        out_specs=(tile, P(None, None, None, SPACE), P(None, None, SPACE), P(None, SPACE)),
        check_vma=False,
    )
```

```python
import jax
import jax.numpy as jnp
from jax import lax
from jax.experimental import pallas as pl
from jax.experimental.pallas import tpu as pltpu
from jax.sharding import Mesh, PartitionSpec as P

epsilon = 1e-06
TIME = ("x", "core")
SPACE = ("y_hi", "z")
GROUP = ("y_lo", "x", "core")
PLANE = ("y_lo", "x", "y_hi")
C = 256
W = 64
FRAMES = 2
ROWS = 2
PIX = FRAMES * ROWS * W
SPACES = 32
MEMBERS = 16
bf16 = jnp.bfloat16
f32 = jnp.float32


def dot(a, b):
    return lax.dot_general(a, b, (((1,), (0,)), ((), ())), preferred_element_type=f32)


def dot_bt(a, b):
    return lax.dot_general(a, b, (((1,), (1,)), ((), ())), preferred_element_type=f32)


def dot_at(a, b):
    return lax.dot_general(a, b, (((0,), (0,)), ((), ())), preferred_element_type=f32)


def column():
    return lax.broadcasted_iota(jnp.int32, (PIX, C), 0) & (W - 1)


def from_left(value):
    return jnp.where(column() == 0, 0.0, pltpu.roll(value, 1, 0))


def from_right(value):
    return jnp.where(column() == W - 1, 0.0, pltpu.roll(value, PIX - 1, 0))


def call(kernel, outs, flops, *operands, **given):
    moved = sum(v.size * v.dtype.itemsize for v in operands)
    moved += sum(s.size * s.dtype.itemsize for s in jax.tree.leaves(outs))
    return pl.pallas_call(
        kernel,
        out_shape=outs,
        compiler_params=pltpu.CompilerParams(vmem_limit_bytes=40 << 20),
        cost_estimate=pl.CostEstimate(flops=flops, bytes_accessed=moved, transcendentals=0),
        **given,
    )(*operands)


def with_scalars(operands):
    specs = [pl.BlockSpec(memory_space=pltpu.SMEM)]
    return specs + [pl.BlockSpec(memory_space=pltpu.VMEM)] * (len(operands) - 1)


def shape(dims, dtype):
    return jax.ShapeDtypeStruct(dims, dtype)


def arranged(cot_ref, up_ref):
    row = lax.broadcasted_iota(jnp.int32, (2 * W, 2 * W), 0)
    col = lax.broadcasted_iota(jnp.int32, (2 * W, 2 * W), 1)
    order = (col == 2 * (row & (W - 1)) + (row >> 6)).astype(f32).astype(bf16)
    for frame in range(FRAMES):
        for height in range(ROWS):
            first = (frame * ROWS + height) * W
            for t in range(2):
                pair = jnp.concatenate(
                    [cot_ref[2 * frame + t, 2 * height + p] for p in range(2)], axis=1
                )
                pair = dot(order, pair).astype(bf16)
                for p in range(2):
                    for q in range(2):
                        up_ref[2 * t + p, first : first + W, q * 128 : q * 128 + 128] = pair[
                            q * W : q * W + W, p * 128 : p * 128 + 128
                        ]


def state_of(up_ref, weight_ref):
    state = None
    for at in range(4):
        part = dot_bt(up_ref[at], weight_ref[:, at * C : at * C + C])
        state = part if state is None else state + part
    return state


def state_kernel(cot_ref, weight_ref, up_ref, state_ref, time_cot_ref):
    arranged(cot_ref, up_ref)
    state = state_of(up_ref, weight_ref)
    state_ref[...] = state
    time_cot_ref[...] = state.astype(bf16)


def later_kernel(cot_ref, weight_ref, up_ref, time_cot_ref):
    arranged(cot_ref, up_ref)
    time_cot_ref[...] = state_of(up_ref, weight_ref).astype(bf16)


def rows_at(block, low, high, offset):
    if offset == 0:
        return block[...].reshape(PIX, C)
    parts = []
    for frame in range(FRAMES):
        if offset < 0:
            parts += [low[frame], block[frame, 0]]
        else:
            parts += [block[frame, 1], high[frame]]
    return jnp.concatenate(parts, axis=0)


def put(core_ref, mine_ref, other_ref, block, start, value):
    first_core = core_ref[0] == 0
    value = value.astype(bf16)
    left, right = value[:, :, :128], value[:, :, 128:]
    count = value.shape[0]
    mine_ref[block, start : start + count] = jnp.where(first_core, left, right)
    other_ref[block, start : start + count] = jnp.where(first_core, right, left)


def paired(one, two):
    return jnp.concatenate([one.reshape(SPACES, 8, C), two.reshape(SPACES, 8, C)], axis=1)


def forward_kernel(
    core_ref, in_ref, low_ref, high_ref, spatial_ref, cot_ref, later_cot_ref, time_ref,
    act_ref, pre_ref, mine_ref, other_ref,
):
    half = ROWS * W
    taps = [None] * 3
    for i in range(3):
        rows = rows_at(in_ref, low_ref, high_ref, i - 1)
        for j in range(3):
            part = dot(rows, spatial_ref[i, j])
            taps[j] = part if taps[j] is None else taps[j] + part
    pre_act = from_left(taps[0]) + taps[1] + from_right(taps[2])
    scale = jnp.sqrt(jnp.mean(pre_act * pre_act, -1, keepdims=True) + epsilon)
    normed = pre_act / scale
    sig = 1.0 / (1.0 + jnp.exp(-normed))
    act_ref[...] = (normed / (1.0 + jnp.exp(-normed))).astype(bf16)
    middle = jnp.concatenate([cot_ref[half:, :], later_cot_ref[:half, :]], axis=0)
    act_grad = dot_bt(cot_ref[...], time_ref[0]) + dot_bt(middle, time_ref[1])
    act_grad = act_grad + dot_bt(later_cot_ref[...], time_ref[2])
    norm_grad = act_grad * sig * (1.0 + normed * (1.0 - sig))
    mean = jnp.mean(norm_grad * normed, -1, keepdims=True)
    pre = ((norm_grad - normed * mean) / scale).astype(bf16)
    pre_ref[...] = pre
    wide = pre.astype(f32)
    shifted = [from_right(wide).astype(bf16), pre, from_left(wide).astype(bf16)]

    def tap(at):
        return dot_at(shifted[at % 3], rows_at(in_ref, low_ref, high_ref, at // 3 - 1))

    for block in range(4):
        value = paired(tap(2 * block), tap(2 * block + 1))
        put(core_ref, mine_ref, other_ref, block, 0, value)


def rest_kernel(
    core_ref, in_ref, high_ref, pre_ref, act_ref, cot_ref, later_cot_ref, up_ref, later_up_ref,
    time_ref, mine_ref, other_ref,
):
    half = ROWS * W
    act = act_ref[...]
    middle = jnp.concatenate([cot_ref[half:, :], later_cot_ref[:half, :]], axis=0)
    last = from_left(pre_ref[...].astype(f32)).astype(bf16)
    value = paired(dot_at(last, rows_at(in_ref, None, high_ref, 1)), dot_at(cot_ref[...], act))
    put(core_ref, mine_ref, other_ref, 0, 0, value)
    value = paired(dot_at(middle, act), dot_at(later_cot_ref[...], act))
    put(core_ref, mine_ref, other_ref, 1, 0, value)
    own = in_ref[...].reshape(PIX, C)
    mixed = [
        (own.astype(f32) + dot(act, time_ref[0])).astype(bf16),
        dot(act, time_ref[1]).astype(bf16),
        dot(act, time_ref[2]).astype(bf16),
    ]
    for at in range(4):
        part = dot_at(up_ref[at], mixed[0])
        part = part + dot_at(up_ref[at, half:, :], mixed[1][:half, :])
        part = part + dot_at(later_up_ref[at, :half, :], mixed[1][half:, :])
        part = part + dot_at(later_up_ref[at], mixed[2])
        part = part.reshape(8, 32, C)
        for low in range(2):
            rows = part[:, low * 16 : low * 16 + 16]
            put(core_ref, mine_ref, other_ref, 2 + low, at * 8, rows)


def swap_sum_kernel(mine_one, mine_two, arrived_one, arrived_two, out_ref, held_ref, sems):
    copies = []
    for at in range(8):
        mine = mine_one if at < 4 else mine_two
        arrived = arrived_one if at < 4 else arrived_two
        total = mine[at % 4].astype(f32) + arrived[at % 4].astype(f32)
        held_ref[at] = total.astype(bf16)
        copies.append(pltpu.make_async_copy(held_ref.at[at], out_ref.at[at], sems.at[at]))
        copies[-1].start()
    for copy in copies:
        copy.wait()


def plane_sum_kernel(parts_ref, out_ref):
    total = parts_ref[0].astype(f32)
    for at in range(1, 16):
        total = total + parts_ref[at].astype(f32)
    out_ref[...] = total.astype(bf16)


def depth_sum_kernel(parts_ref, out_ref):
    total = parts_ref[0].astype(f32)
    for at in range(1, 16):
        total = total + parts_ref[at].astype(f32)
    for at in range(MEMBERS):
        out_ref[at] = total


def input_grad_kernel(state_ref, pre_ref, low_ref, high_ref, weight_ref, out_ref):
    taps = [None] * 3
    for i in range(3):
        rows = rows_at(pre_ref, low_ref, high_ref, 1 - i)
        for j in range(3):
            part = dot_bt(rows, weight_ref[i, j])
            taps[j] = part if taps[j] is None else taps[j] + part
    total = state_ref[...] + (from_right(taps[0]) + taps[1] + from_left(taps[2]))
    out_ref[...] = total.astype(bf16)


def unpack_kernel(in_ref, spatial_ref, time_ref, up_ref):
    for block in range(6):
        for lane in range(2):
            for low in range(2):
                at = 2 * block + low
                value = in_ref[2 * block + lane, low * 8 : low * 8 + 8, :]
                if at < 9:
                    spatial_ref[at, :, lane * 128 : lane * 128 + 128] = value
                else:
                    time_ref[at - 9, :, lane * 128 : lane * 128 + 128] = value
    for low in range(2):
        for lane in range(2):
            up_ref[low * 16 : low * 16 + 16, lane * 128 : lane * 128 + 128] = in_ref[
                12 + 2 * low + lane
            ]


def states(cotangent, up_weight):
    outs = (shape((4, PIX, C), bf16), shape((PIX, C), f32), shape((PIX, C), bf16))
    return call(state_kernel, outs, 10 * PIX * C * C, cotangent, up_weight)


def later_states(cotangent, up_weight):
    outs = (shape((4, PIX, C), bf16), shape((PIX, C), bf16))
    return call(later_kernel, outs, 10 * PIX * C * C, cotangent, up_weight)


def forward(*operands):
    flat, half = shape((PIX, C), bf16), shape((4, SPACES, 16, 128), bf16)
    specs = with_scalars(operands)
    outs = (flat, flat, half, half)
    return call(forward_kernel, outs, 40 * PIX * C * C, *operands, in_specs=specs)


def rest(*operands):
    half = shape((4, SPACES, 16, 128), bf16)
    specs = with_scalars(operands)
    return call(rest_kernel, (half, half), 38 * PIX * C * C, *operands, in_specs=specs)


def swap_sum(*operands):
    out = shape((8, SPACES, 16, 128), bf16)
    return call(
        swap_sum_kernel,
        out,
        0,
        *operands,
        out_specs=pl.BlockSpec(memory_space=pl.ANY),
        scratch_shapes=[pltpu.VMEM(out.shape, bf16), pltpu.SemaphoreType.DMA((8,))],
    )


def input_gradient(*operands):
    outs = (shape((PIX, C), bf16),)
    return call(input_grad_kernel, outs, 18 * PIX * C * C, *operands)[0]


def unpacked(gathered):
    outs = (shape((9, 8, C), f32), shape((3, 8, C), f32), shape((32, C), f32))
    return call(unpack_kernel, outs, 0, gathered)


def halo(block, after):
    even = (lax.axis_index(SPACE) & 1) == 0
    top, bottom = block[:, 0], block[:, ROWS - 1]
    pairs = [[(i, i + 1) for i in range(start, SPACES - 1, 2)] for start in (0, 1)]
    pairs = [found + [(b, a) for a, b in found] for found in pairs]
    first = lax.ppermute(jnp.where(even, bottom, top), SPACE, pairs[0])
    second = lax.ppermute(jnp.where(even, top, bottom), SPACE, pairs[1])
    first, second, after = lax.optimization_barrier((first, second, after))
    return jnp.where(even, second, first), jnp.where(even, first, second), after


def local(inputs, cotangent, spatial_weight, time_weight, up_weight):
    tile = inputs.reshape(FRAMES, ROWS, W, C)
    cotangent = cotangent.reshape(2 * FRAMES, 2 * ROWS, 2 * W, -1)
    later = lax.ppermute(cotangent, TIME, [(i + 1, i) for i in range(7)])
    upward, state_grad, time_cot = states(cotangent, up_weight)
    later, time_cot = lax.optimization_barrier((later, time_cot))
    later_up, later_cot = later_states(later, up_weight)
    low, high, later_cot = halo(tile, later_cot)
    core = lax.axis_index("core").astype(jnp.int32).reshape(1)
    activated, pre_grad, mine_one, other_one = forward(
        core, tile, low, high, spatial_weight, time_cot, later_cot, time_weight
    )
    other_one = lax.ppermute(other_one, "core", [(0, 1), (1, 0)])
    mine_two, other_two = rest(
        core, tile, high, pre_grad, activated, time_cot, later_cot, upward, later_up, time_weight
    )
    other_one, other_two = lax.optimization_barrier((other_one, other_two))
    other_two = lax.ppermute(other_two, "core", [(0, 1), (1, 0)])
    value = swap_sum(mine_one, mine_two, other_one, other_two)
    pre_tile = pre_grad.reshape(FRAMES, ROWS, W, C)
    held, value = lax.optimization_barrier((pre_tile, value))
    value = lax.all_to_all(value.reshape(16, 16, 16, 128), PLANE, 0, 0)
    pre_low, pre_high, state_grad = halo(held, state_grad)
    input_grad = input_gradient(state_grad, pre_tile, pre_low, pre_high, spatial_weight)
    value, input_grad = lax.optimization_barrier((value, input_grad))
    value = call(plane_sum_kernel, (shape((16, 16, 128), bf16),), 0, value)[0]
    value = lax.all_to_all(value, "z", 0, 0)
    value = call(depth_sum_kernel, (shape((MEMBERS, 16, 128), f32),), 0, value)[0]
    spatial_grad, time_grad, up_grad = unpacked(lax.all_to_all(value, GROUP, 0, 0))
    return (
        input_grad.reshape(inputs.shape),
        jnp.swapaxes(spatial_grad.reshape(3, 3, 8, C), 2, 3),
        jnp.swapaxes(time_grad, 1, 2),
        jnp.swapaxes(up_grad, 0, 1),
    )


def solution(mesh):
    whole = Mesh(mesh.devices.reshape(2, 4, 2, 2, 16), ("y_lo", "x", "core", "y_hi", "z"))
    tile = P("y_lo", TIME, SPACE, None, None)
    return jax.shard_map(
        local,
        mesh=whole,
        in_specs=(tile, tile, P(), P(), P()),
        out_specs=(tile, P(None, None, None, SPACE), P(None, None, SPACE), P(None, SPACE)),
        check_vma=False,
    )
```

```python
import jax
import jax.numpy as jnp
from jax import lax
from jax.experimental import pallas as pl
from jax.experimental.pallas import tpu as pltpu
from jax.sharding import Mesh, PartitionSpec as P

epsilon = 1e-06
TIME = ("x", "core")
SPACE = ("y_hi", "z")
GROUP = ("y_lo", "x", "core")
PLANE = ("y_lo", "x", "y_hi")
C = 256
W = 64
FRAMES = 2
ROWS = 2
PIX = FRAMES * ROWS * W
SPACES = 32
MEMBERS = 16
bf16 = jnp.bfloat16
f32 = jnp.float32


def dot(a, b):
    return lax.dot_general(a, b, (((1,), (0,)), ((), ())), preferred_element_type=f32)


def dot_bt(a, b):
    return lax.dot_general(a, b, (((1,), (1,)), ((), ())), preferred_element_type=f32)


def dot_at(a, b):
    return lax.dot_general(a, b, (((0,), (0,)), ((), ())), preferred_element_type=f32)


def column():
    return lax.broadcasted_iota(jnp.int32, (PIX, C), 0) & (W - 1)


def from_left(value):
    return jnp.where(column() == 0, 0.0, pltpu.roll(value, 1, 0))


def from_right(value):
    return jnp.where(column() == W - 1, 0.0, pltpu.roll(value, PIX - 1, 0))


def call(kernel, outs, flops, *operands, **given):
    moved = sum(v.size * v.dtype.itemsize for v in operands)
    moved += sum(s.size * s.dtype.itemsize for s in jax.tree.leaves(outs))
    return pl.pallas_call(
        kernel,
        out_shape=outs,
        compiler_params=pltpu.CompilerParams(vmem_limit_bytes=40 << 20),
        cost_estimate=pl.CostEstimate(flops=flops, bytes_accessed=moved, transcendentals=0),
        **given,
    )(*operands)


def with_scalars(operands):
    specs = [pl.BlockSpec(memory_space=pltpu.SMEM)]
    return specs + [pl.BlockSpec(memory_space=pltpu.VMEM)] * (len(operands) - 1)


def shape(dims, dtype):
    return jax.ShapeDtypeStruct(dims, dtype)


def arranged(cot_ref, up_ref):
    row = lax.broadcasted_iota(jnp.int32, (2 * W, 2 * W), 0)
    col = lax.broadcasted_iota(jnp.int32, (2 * W, 2 * W), 1)
    order = (col == 2 * (row & (W - 1)) + (row >> 6)).astype(f32).astype(bf16)
    for frame in range(FRAMES):
        for height in range(ROWS):
            first = (frame * ROWS + height) * W
            for t in range(2):
                pair = jnp.concatenate(
                    [cot_ref[2 * frame + t, 2 * height + p] for p in range(2)], axis=1
                )
                pair = dot(order, pair).astype(bf16)
                for p in range(2):
                    for q in range(2):
                        up_ref[2 * t + p, first : first + W, q * 128 : q * 128 + 128] = pair[
                            q * W : q * W + W, p * 128 : p * 128 + 128
                        ]


def state_of(up_ref, weight_ref):
    state = None
    for at in range(4):
        part = dot_bt(up_ref[at], weight_ref[:, at * C : at * C + C])
        state = part if state is None else state + part
    return state


def own_kernel(cot_ref, up_ref):
    arranged(cot_ref, up_ref)


def state_kernel(
    cot_ref, up_ref, weight_ref, later_up_ref, state_ref, time_cot_ref, later_cot_ref
):
    state = state_of(up_ref, weight_ref)
    state_ref[...] = state
    time_cot_ref[...] = state.astype(bf16)
    arranged(cot_ref, later_up_ref)
    later_cot_ref[...] = state_of(later_up_ref, weight_ref).astype(bf16)


def rows_at(block, low, high, offset):
    if offset == 0:
        return block[...].reshape(PIX, C)
    parts = []
    for frame in range(FRAMES):
        if offset < 0:
            parts += [low[frame], block[frame, 0]]
        else:
            parts += [block[frame, 1], high[frame]]
    return jnp.concatenate(parts, axis=0)


def put(core_ref, mine_ref, other_ref, block, start, value):
    first_core = core_ref[0] == 0
    value = value.astype(bf16)
    left, right = value[:, :, :128], value[:, :, 128:]
    count = value.shape[0]
    mine_ref[block, start : start + count] = jnp.where(first_core, left, right)
    other_ref[block, start : start + count] = jnp.where(first_core, right, left)


def paired(one, two):
    return jnp.concatenate([one.reshape(SPACES, 8, C), two.reshape(SPACES, 8, C)], axis=1)


def gradients_kernel(
    core_ref, in_ref, low_ref, high_ref, spatial_ref, cot_ref, later_cot_ref, up_ref, later_up_ref,
    time_ref, pre_ref, mine_ref, other_ref,
):
    half = ROWS * W
    taps = [None] * 3
    for i in range(3):
        rows = rows_at(in_ref, low_ref, high_ref, i - 1)
        for j in range(3):
            part = dot(rows, spatial_ref[i, j])
            taps[j] = part if taps[j] is None else taps[j] + part
    pre_act = from_left(taps[0]) + taps[1] + from_right(taps[2])
    scale = jnp.sqrt(jnp.mean(pre_act * pre_act, -1, keepdims=True) + epsilon)
    normed = pre_act / scale
    sig = 1.0 / (1.0 + jnp.exp(-normed))
    act = (normed / (1.0 + jnp.exp(-normed))).astype(bf16)
    middle = jnp.concatenate([cot_ref[half:, :], later_cot_ref[:half, :]], axis=0)
    act_grad = dot_bt(cot_ref[...], time_ref[0]) + dot_bt(middle, time_ref[1])
    act_grad = act_grad + dot_bt(later_cot_ref[...], time_ref[2])
    norm_grad = act_grad * sig * (1.0 + normed * (1.0 - sig))
    mean = jnp.mean(norm_grad * normed, -1, keepdims=True)
    pre = ((norm_grad - normed * mean) / scale).astype(bf16)
    pre_ref[...] = pre
    wide = pre.astype(f32)
    shifted = [from_right(wide).astype(bf16), pre, from_left(wide).astype(bf16)]

    cots = [cot_ref[...], middle, later_cot_ref[...]]

    def tap(at):
        if at < 9:
            return dot_at(shifted[at % 3], rows_at(in_ref, low_ref, high_ref, at // 3 - 1))
        return dot_at(cots[at - 9], act)

    for block in range(6):
        value = paired(tap(2 * block), tap(2 * block + 1))
        put(core_ref, mine_ref, other_ref, block, 0, value)
    own = in_ref[...].reshape(PIX, C)
    mixed = [
        (own.astype(f32) + dot(act, time_ref[0])).astype(bf16),
        dot(act, time_ref[1]).astype(bf16),
        dot(act, time_ref[2]).astype(bf16),
    ]
    for at in range(4):
        part = dot_at(up_ref[at], mixed[0])
        part = part + dot_at(up_ref[at, half:, :], mixed[1][:half, :])
        part = part + dot_at(later_up_ref[at, :half, :], mixed[1][half:, :])
        part = part + dot_at(later_up_ref[at], mixed[2])
        part = part.reshape(8, 32, C)
        for low in range(2):
            rows = part[:, low * 16 : low * 16 + 16]
            put(core_ref, mine_ref, other_ref, 6 + low, at * 8, rows)


def swap_sum_kernel(mine_ref, arrived_ref, out_ref, held_ref, sems):
    copies = []
    for at in range(8):
        total = mine_ref[at].astype(f32) + arrived_ref[at].astype(f32)
        held_ref[at] = total.astype(bf16)
        copies.append(pltpu.make_async_copy(held_ref.at[at], out_ref.at[at], sems.at[at]))
        copies[-1].start()
    for copy in copies:
        copy.wait()


def plane_sum_kernel(parts_ref, out_ref):
    total = parts_ref[0].astype(f32)
    for at in range(1, 16):
        total = total + parts_ref[at].astype(f32)
    out_ref[...] = total.astype(bf16)


def depth_sum_kernel(parts_ref, out_ref):
    total = parts_ref[0].astype(f32)
    for at in range(1, 16):
        total = total + parts_ref[at].astype(f32)
    for at in range(MEMBERS):
        out_ref[at] = total


def input_grad_kernel(state_ref, pre_ref, low_ref, high_ref, weight_ref, out_ref):
    taps = [None] * 3
    for i in range(3):
        rows = rows_at(pre_ref, low_ref, high_ref, 1 - i)
        for j in range(3):
            part = dot_bt(rows, weight_ref[i, j])
            taps[j] = part if taps[j] is None else taps[j] + part
    total = state_ref[...] + (from_right(taps[0]) + taps[1] + from_left(taps[2]))
    out_ref[...] = total.astype(bf16)


def unpack_kernel(in_ref, spatial_ref, time_ref, up_ref):
    for block in range(6):
        for lane in range(2):
            for low in range(2):
                at = 2 * block + low
                value = in_ref[2 * block + lane, low * 8 : low * 8 + 8, :]
                if at < 9:
                    spatial_ref[at, :, lane * 128 : lane * 128 + 128] = value
                else:
                    time_ref[at - 9, :, lane * 128 : lane * 128 + 128] = value
    for low in range(2):
        for lane in range(2):
            up_ref[low * 16 : low * 16 + 16, lane * 128 : lane * 128 + 128] = in_ref[
                12 + 2 * low + lane
            ]


def own_upward(cotangent):
    return call(own_kernel, (shape((4, PIX, C), bf16),), 2 * PIX * C * C, cotangent)[0]


def states(later, upward, up_weight):
    flat = shape((PIX, C), bf16)
    outs = (shape((4, PIX, C), bf16), shape((PIX, C), f32), flat, flat)
    return call(state_kernel, outs, 18 * PIX * C * C, later, upward, up_weight)


def gradients(*operands):
    half = shape((8, SPACES, 16, 128), bf16)
    specs = with_scalars(operands)
    outs = (shape((PIX, C), bf16), half, half)
    return call(gradients_kernel, outs, 76 * PIX * C * C, *operands, in_specs=specs)


def swap_sum(*operands):
    out = shape((8, SPACES, 16, 128), bf16)
    return call(
        swap_sum_kernel,
        out,
        0,
        *operands,
        out_specs=pl.BlockSpec(memory_space=pl.ANY),
        scratch_shapes=[pltpu.VMEM(out.shape, bf16), pltpu.SemaphoreType.DMA((8,))],
    )


def input_gradient(*operands):
    outs = (shape((PIX, C), bf16),)
    return call(input_grad_kernel, outs, 18 * PIX * C * C, *operands)[0]


def unpacked(gathered):
    outs = (shape((9, 8, C), f32), shape((3, 8, C), f32), shape((32, C), f32))
    return call(unpack_kernel, outs, 0, gathered)


def halo(block, after):
    even = (lax.axis_index(SPACE) & 1) == 0
    top, bottom = block[:, 0], block[:, ROWS - 1]
    pairs = [[(i, i + 1) for i in range(start, SPACES - 1, 2)] for start in (0, 1)]
    pairs = [found + [(b, a) for a, b in found] for found in pairs]
    first = lax.ppermute(jnp.where(even, bottom, top), SPACE, pairs[0])
    second = lax.ppermute(jnp.where(even, top, bottom), SPACE, pairs[1])
    first, second, after = lax.optimization_barrier((first, second, after))
    return jnp.where(even, second, first), jnp.where(even, first, second), after


def local(inputs, cotangent, spatial_weight, time_weight, up_weight):
    tile = inputs.reshape(FRAMES, ROWS, W, C)
    cotangent = cotangent.reshape(2 * FRAMES, 2 * ROWS, 2 * W, -1)
    later = lax.ppermute(cotangent, TIME, [(i + 1, i) for i in range(7)])
    upward = own_upward(cotangent)
    later, upward = lax.optimization_barrier((later, upward))
    later_up, state_grad, time_cot, later_cot = states(later, upward, up_weight)
    low, high, later_cot = halo(tile, later_cot)
    core = lax.axis_index("core").astype(jnp.int32).reshape(1)
    pre_grad, mine, other = gradients(
        core, tile, low, high, spatial_weight, time_cot, later_cot, upward, later_up, time_weight
    )
    other = lax.ppermute(other, "core", [(0, 1), (1, 0)])
    value = swap_sum(mine, other)
    pre_tile = pre_grad.reshape(FRAMES, ROWS, W, C)
    held, value = lax.optimization_barrier((pre_tile, value))
    value = lax.all_to_all(value.reshape(16, 16, 16, 128), PLANE, 0, 0)
    pre_low, pre_high, state_grad = halo(held, state_grad)
    input_grad = input_gradient(state_grad, pre_tile, pre_low, pre_high, spatial_weight)
    value, input_grad = lax.optimization_barrier((value, input_grad))
    value = call(plane_sum_kernel, (shape((16, 16, 128), bf16),), 0, value)[0]
    value = lax.all_to_all(value, "z", 0, 0)
    value = call(depth_sum_kernel, (shape((MEMBERS, 16, 128), f32),), 0, value)[0]
    spatial_grad, time_grad, up_grad = unpacked(lax.all_to_all(value, GROUP, 0, 0))
    return (
        input_grad.reshape(inputs.shape),
        jnp.swapaxes(spatial_grad.reshape(3, 3, 8, C), 2, 3),
        jnp.swapaxes(time_grad, 1, 2),
        jnp.swapaxes(up_grad, 0, 1),
    )


def solution(mesh):
    whole = Mesh(mesh.devices.reshape(2, 4, 2, 2, 16), ("y_lo", "x", "core", "y_hi", "z"))
    tile = P("y_lo", TIME, SPACE, None, None)
    return jax.shard_map(
        local,
        mesh=whole,
        in_specs=(tile, tile, P(), P(), P()),
        out_specs=(tile, P(None, None, None, SPACE), P(None, None, SPACE), P(None, SPACE)),
        check_vma=False,
    )
```

```python
import jax
import jax.numpy as jnp
from jax import lax
from jax.experimental import pallas as pl
from jax.experimental.pallas import tpu as pltpu
from jax.sharding import Mesh, PartitionSpec as P

epsilon = 1e-06
TIME = ("x", "core")
SPACE = ("y_hi", "z_hi", "z_lo")
GROUP = ("y_lo", "x", "core")
NEAR = ("y_lo", "x", "y_hi", "z_lo")
C = 256
W = 64
FRAMES = 2
ROWS = 2
PIX = FRAMES * ROWS * W
SPACES = 32
MEMBERS = 16
bf16 = jnp.bfloat16
f32 = jnp.float32


def dot(a, b):
    return lax.dot_general(a, b, (((1,), (0,)), ((), ())), preferred_element_type=f32)


def dot_bt(a, b):
    return lax.dot_general(a, b, (((1,), (1,)), ((), ())), preferred_element_type=f32)


def dot_at(a, b):
    return lax.dot_general(a, b, (((0,), (0,)), ((), ())), preferred_element_type=f32)


def column():
    return lax.broadcasted_iota(jnp.int32, (PIX, C), 0) & (W - 1)


def from_left(value):
    return jnp.where(column() == 0, 0.0, pltpu.roll(value, 1, 0))


def from_right(value):
    return jnp.where(column() == W - 1, 0.0, pltpu.roll(value, PIX - 1, 0))


def call(kernel, outs, flops, *operands, **given):
    moved = sum(v.size * v.dtype.itemsize for v in operands)
    moved += sum(s.size * s.dtype.itemsize for s in jax.tree.leaves(outs))
    return pl.pallas_call(
        kernel,
        out_shape=outs,
        compiler_params=pltpu.CompilerParams(vmem_limit_bytes=40 << 20),
        cost_estimate=pl.CostEstimate(flops=flops, bytes_accessed=moved, transcendentals=0),
        **given,
    )(*operands)


def with_scalars(operands):
    specs = [pl.BlockSpec(memory_space=pltpu.SMEM)]
    return specs + [pl.BlockSpec(memory_space=pltpu.VMEM)] * (len(operands) - 1)


def shape(dims, dtype):
    return jax.ShapeDtypeStruct(dims, dtype)


def arranged(cot_ref, up_ref):
    row = lax.broadcasted_iota(jnp.int32, (2 * W, 2 * W), 0)
    col = lax.broadcasted_iota(jnp.int32, (2 * W, 2 * W), 1)
    order = (col == 2 * (row & (W - 1)) + (row >> 6)).astype(f32).astype(bf16)
    for frame in range(FRAMES):
        for height in range(ROWS):
            first = (frame * ROWS + height) * W
            for t in range(2):
                pair = jnp.concatenate(
                    [cot_ref[2 * frame + t, 2 * height + p] for p in range(2)], axis=1
                )
                pair = dot(order, pair).astype(bf16)
                for p in range(2):
                    for q in range(2):
                        up_ref[2 * t + p, first : first + W, q * 128 : q * 128 + 128] = pair[
                            q * W : q * W + W, p * 128 : p * 128 + 128
                        ]


def state_of(up_ref, weight_ref):
    state = None
    for at in range(4):
        part = dot_bt(up_ref[at], weight_ref[:, at * C : at * C + C])
        state = part if state is None else state + part
    return state


def own_kernel(cot_ref, up_ref):
    arranged(cot_ref, up_ref)


def state_kernel(
    cot_ref, up_ref, weight_ref, later_up_ref, state_ref, time_cot_ref, later_cot_ref
):
    state = state_of(up_ref, weight_ref)
    state_ref[...] = state
    time_cot_ref[...] = state.astype(bf16)
    arranged(cot_ref, later_up_ref)
    later_cot_ref[...] = state_of(later_up_ref, weight_ref).astype(bf16)


def rows_at(block, low, high, offset):
    if offset == 0:
        return block[...].reshape(PIX, C)
    parts = []
    for frame in range(FRAMES):
        if offset < 0:
            parts += [low[frame], block[frame, 0]]
        else:
            parts += [block[frame, 1], high[frame]]
    return jnp.concatenate(parts, axis=0)


def put(core_ref, mine_ref, other_ref, block, start, value):
    first_core = core_ref[0] == 0
    value = value.astype(bf16)
    left, right = value[:, :, :128], value[:, :, 128:]
    count = value.shape[0]
    mine_ref[block, start : start + count] = jnp.where(first_core, left, right)
    other_ref[block, start : start + count] = jnp.where(first_core, right, left)


def paired(one, two):
    return jnp.concatenate([one.reshape(SPACES, 8, C), two.reshape(SPACES, 8, C)], axis=1)


def gradients_kernel(
    core_ref, in_ref, low_ref, high_ref, spatial_ref, cot_ref, later_cot_ref, up_ref, later_up_ref,
    time_ref, pre_ref, mine_ref, other_ref,
):
    half = ROWS * W
    taps = [None] * 3
    for i in range(3):
        rows = rows_at(in_ref, low_ref, high_ref, i - 1)
        for j in range(3):
            part = dot(rows, spatial_ref[i, j])
            taps[j] = part if taps[j] is None else taps[j] + part
    pre_act = from_left(taps[0]) + taps[1] + from_right(taps[2])
    scale = jnp.sqrt(jnp.mean(pre_act * pre_act, -1, keepdims=True) + epsilon)
    normed = pre_act / scale
    sig = 1.0 / (1.0 + jnp.exp(-normed))
    act = (normed / (1.0 + jnp.exp(-normed))).astype(bf16)
    middle = jnp.concatenate([cot_ref[half:, :], later_cot_ref[:half, :]], axis=0)
    act_grad = dot_bt(cot_ref[...], time_ref[0]) + dot_bt(middle, time_ref[1])
    act_grad = act_grad + dot_bt(later_cot_ref[...], time_ref[2])
    norm_grad = act_grad * sig * (1.0 + normed * (1.0 - sig))
    mean = jnp.mean(norm_grad * normed, -1, keepdims=True)
    pre = ((norm_grad - normed * mean) / scale).astype(bf16)
    pre_ref[...] = pre
    wide = pre.astype(f32)
    shifted = [from_right(wide).astype(bf16), pre, from_left(wide).astype(bf16)]

    cots = [cot_ref[...], middle, later_cot_ref[...]]

    def tap(at):
        if at < 9:
            return dot_at(shifted[at % 3], rows_at(in_ref, low_ref, high_ref, at // 3 - 1))
        return dot_at(cots[at - 9], act)

    for block in range(6):
        value = paired(tap(2 * block), tap(2 * block + 1))
        put(core_ref, mine_ref, other_ref, block, 0, value)
    own = in_ref[...].reshape(PIX, C)
    mixed = [
        (own.astype(f32) + dot(act, time_ref[0])).astype(bf16),
        dot(act, time_ref[1]).astype(bf16),
        dot(act, time_ref[2]).astype(bf16),
    ]
    for at in range(4):
        part = dot_at(up_ref[at], mixed[0])
        part = part + dot_at(up_ref[at, half:, :], mixed[1][:half, :])
        part = part + dot_at(later_up_ref[at, :half, :], mixed[1][half:, :])
        part = part + dot_at(later_up_ref[at], mixed[2])
        part = part.reshape(8, 32, C)
        for low in range(2):
            rows = part[:, low * 16 : low * 16 + 16]
            put(core_ref, mine_ref, other_ref, 6 + low, at * 8, rows)


def swap_sum_kernel(mine_ref, arrived_ref, out_ref, held_ref, sems):
    copies = []
    for at in range(8):
        total = (mine_ref[at] + arrived_ref[at]).reshape(2, 8, 2, 16, 128)
        for low in range(2):
            held_ref[at, :, low] = total[:, :, low]
        copies.append(pltpu.make_async_copy(held_ref.at[at], out_ref.at[at], sems.at[at]))
        copies[-1].start()
    for copy in copies:
        copy.wait()


def total_of(parts_ref):
    total = parts_ref[0].astype(f32)
    for at in range(1, parts_ref.shape[0]):
        total = total + parts_ref[at].astype(f32)
    return total


def near_sum_kernel(parts_ref, out_ref):
    out_ref[...] = total_of(parts_ref).astype(bf16)


def far_sum_kernel(parts_ref, out_ref):
    total = total_of(parts_ref)
    for at in range(MEMBERS):
        out_ref[at] = total


def input_grad_kernel(state_ref, pre_ref, low_ref, high_ref, weight_ref, out_ref):
    taps = [None] * 3
    for i in range(3):
        rows = rows_at(pre_ref, low_ref, high_ref, 1 - i)
        for j in range(3):
            part = dot_bt(rows, weight_ref[i, j])
            taps[j] = part if taps[j] is None else taps[j] + part
    total = state_ref[...] + (from_right(taps[0]) + taps[1] + from_left(taps[2]))
    out_ref[...] = total.astype(bf16)


def unpack_kernel(in_ref, spatial_ref, time_ref, up_ref):
    for block in range(6):
        for lane in range(2):
            for low in range(2):
                at = 2 * block + low
                value = in_ref[2 * block + lane, low * 8 : low * 8 + 8, :]
                if at < 9:
                    spatial_ref[at, :, lane * 128 : lane * 128 + 128] = value
                else:
                    time_ref[at - 9, :, lane * 128 : lane * 128 + 128] = value
    for low in range(2):
        for lane in range(2):
            up_ref[low * 16 : low * 16 + 16, lane * 128 : lane * 128 + 128] = in_ref[
                12 + 2 * low + lane
            ]


def own_upward(cotangent):
    return call(own_kernel, (shape((4, PIX, C), bf16),), 2 * PIX * C * C, cotangent)[0]


def states(later, upward, up_weight):
    flat = shape((PIX, C), bf16)
    outs = (shape((4, PIX, C), bf16), shape((PIX, C), f32), flat, flat)
    return call(state_kernel, outs, 18 * PIX * C * C, later, upward, up_weight)


def gradients(*operands):
    half = shape((8, SPACES, 16, 128), bf16)
    specs = with_scalars(operands)
    outs = (shape((PIX, C), bf16), half, half)
    return call(gradients_kernel, outs, 76 * PIX * C * C, *operands, in_specs=specs)


def swap_sum(*operands):
    out = shape((8, 2, 2, 8, 16, 128), bf16)
    return call(
        swap_sum_kernel,
        out,
        0,
        *operands,
        out_specs=pl.BlockSpec(memory_space=pl.ANY),
        scratch_shapes=[pltpu.VMEM(out.shape, bf16), pltpu.SemaphoreType.DMA((8,))],
    )


def input_gradient(*operands):
    outs = (shape((PIX, C), bf16),)
    return call(input_grad_kernel, outs, 18 * PIX * C * C, *operands)[0]


def unpacked(gathered):
    outs = (shape((9, 8, C), f32), shape((3, 8, C), f32), shape((32, C), f32))
    return call(unpack_kernel, outs, 0, gathered)


def halo(block, after):
    even = (lax.axis_index(SPACE) & 1) == 0
    top, bottom = block[:, 0], block[:, ROWS - 1]
    pairs = [[(i, i + 1) for i in range(start, SPACES - 1, 2)] for start in (0, 1)]
    pairs = [found + [(b, a) for a, b in found] for found in pairs]
    first = lax.ppermute(jnp.where(even, bottom, top), SPACE, pairs[0])
    second = lax.ppermute(jnp.where(even, top, bottom), SPACE, pairs[1])
    first, second, after = lax.optimization_barrier((first, second, after))
    return jnp.where(even, second, first), jnp.where(even, first, second), after


def local(inputs, cotangent, spatial_weight, time_weight, up_weight):
    tile = inputs.reshape(FRAMES, ROWS, W, C)
    cotangent = cotangent.reshape(2 * FRAMES, 2 * ROWS, 2 * W, -1)
    later = lax.ppermute(cotangent, TIME, [(i + 1, i) for i in range(7)])
    upward = own_upward(cotangent)
    later, upward = lax.optimization_barrier((later, upward))
    later_up, state_grad, time_cot, later_cot = states(later, upward, up_weight)
    low, high, later_cot = halo(tile, later_cot)
    core = lax.axis_index("core").astype(jnp.int32).reshape(1)
    pre_grad, mine, other = gradients(
        core, tile, low, high, spatial_weight, time_cot, later_cot, upward, later_up, time_weight
    )
    other = lax.ppermute(other, "core", [(0, 1), (1, 0)])
    value = swap_sum(mine, other)
    pre_tile = pre_grad.reshape(FRAMES, ROWS, W, C)
    held, value = lax.optimization_barrier((pre_tile, value))
    value = lax.all_to_all(value.reshape(32, 8, 16, 128), NEAR, 0, 0)
    pre_low, pre_high, state_grad = halo(held, state_grad)
    input_grad = input_gradient(state_grad, pre_tile, pre_low, pre_high, spatial_weight)
    value, input_grad = lax.optimization_barrier((value, input_grad))
    value = call(near_sum_kernel, (shape((8, 16, 128), bf16),), 0, value)[0]
    value = lax.all_to_all(value, "z_hi", 0, 0)
    value = call(far_sum_kernel, (shape((MEMBERS, 16, 128), f32),), 0, value)[0]
    spatial_grad, time_grad, up_grad = unpacked(lax.all_to_all(value, GROUP, 0, 0))
    return (
        input_grad.reshape(inputs.shape),
        jnp.swapaxes(spatial_grad.reshape(3, 3, 8, C), 2, 3),
        jnp.swapaxes(time_grad, 1, 2),
        jnp.swapaxes(up_grad, 0, 1),
    )


def solution(mesh):
    whole = Mesh(
        mesh.devices.reshape(2, 4, 2, 2, 8, 2), ("y_lo", "x", "core", "y_hi", "z_hi", "z_lo")
    )
    tile = P("y_lo", TIME, SPACE, None, None)
    return jax.shard_map(
        local,
        mesh=whole,
        in_specs=(tile, tile, P(), P(), P()),
        out_specs=(tile, P(None, None, None, SPACE), P(None, None, SPACE), P(None, SPACE)),
        check_vma=False,
    )
```

```python
import jax
import jax.numpy as jnp
from jax import lax
from jax.experimental import pallas as pl
from jax.experimental.pallas import tpu as pltpu
from jax.sharding import Mesh, PartitionSpec as P

epsilon = 1e-06
TIME = ("x", "core")
SPACE = ("y_hi", "z_hi", "z_lo")
GROUP = ("y_lo", "x", "core")
NEAR = ("y_lo", "x", "y_hi", "z_lo")
C = 256
W = 64
FRAMES = 2
ROWS = 2
PIX = FRAMES * ROWS * W
SPACES = 32
MEMBERS = 16
bf16 = jnp.bfloat16
f32 = jnp.float32


def dot(a, b):
    return lax.dot_general(a, b, (((1,), (0,)), ((), ())), preferred_element_type=f32)


def dot_bt(a, b):
    return lax.dot_general(a, b, (((1,), (1,)), ((), ())), preferred_element_type=f32)


def dot_at(a, b):
    return lax.dot_general(a, b, (((0,), (0,)), ((), ())), preferred_element_type=f32)


def column():
    return lax.broadcasted_iota(jnp.int32, (PIX, C), 0) & (W - 1)


def from_left(value):
    return jnp.where(column() == 0, 0.0, pltpu.roll(value, 1, 0))


def from_right(value):
    return jnp.where(column() == W - 1, 0.0, pltpu.roll(value, PIX - 1, 0))


def call(kernel, outs, flops, *operands, **given):
    moved = sum(v.size * v.dtype.itemsize for v in operands)
    moved += sum(s.size * s.dtype.itemsize for s in jax.tree.leaves(outs))
    return pl.pallas_call(
        kernel,
        out_shape=outs,
        compiler_params=pltpu.CompilerParams(vmem_limit_bytes=40 << 20),
        cost_estimate=pl.CostEstimate(flops=flops, bytes_accessed=moved, transcendentals=0),
        **given,
    )(*operands)


def with_scalars(operands):
    specs = [pl.BlockSpec(memory_space=pltpu.SMEM)]
    return specs + [pl.BlockSpec(memory_space=pltpu.VMEM)] * (len(operands) - 1)


def shape(dims, dtype):
    return jax.ShapeDtypeStruct(dims, dtype)


def arranged(cot_ref, up_ref):
    row = lax.broadcasted_iota(jnp.int32, (2 * W, 2 * W), 0)
    col = lax.broadcasted_iota(jnp.int32, (2 * W, 2 * W), 1)
    order = (col == 2 * (row & (W - 1)) + (row >> 6)).astype(f32).astype(bf16)
    for frame in range(FRAMES):
        for height in range(ROWS):
            first = (frame * ROWS + height) * W
            for t in range(2):
                pair = jnp.concatenate(
                    [cot_ref[2 * frame + t, 2 * height + p] for p in range(2)], axis=1
                )
                pair = dot(order, pair).astype(bf16)
                for p in range(2):
                    for q in range(2):
                        up_ref[2 * t + p, first : first + W, q * 128 : q * 128 + 128] = pair[
                            q * W : q * W + W, p * 128 : p * 128 + 128
                        ]


def state_of(up_ref, weight_ref):
    state = None
    for at in range(4):
        part = dot_bt(up_ref[at], weight_ref[:, at * C : at * C + C])
        state = part if state is None else state + part
    return state


def own_kernel(cot_ref, up_ref):
    arranged(cot_ref, up_ref)


def state_kernel(
    cot_ref, up_ref, weight_ref, time_ref, later_up_ref, state_ref, act_grad_ref, time_cot_ref,
    later_cot_ref,
):
    state = state_of(up_ref, weight_ref)
    state_ref[...] = state
    time_cot_ref[...] = state.astype(bf16)
    arranged(cot_ref, later_up_ref)
    later_cot_ref[...] = state_of(later_up_ref, weight_ref).astype(bf16)
    cots = shifted_cots(time_cot_ref, later_cot_ref)
    act_grad = dot_bt(cots[0], time_ref[0]) + dot_bt(cots[1], time_ref[1])
    act_grad_ref[...] = act_grad + dot_bt(cots[2], time_ref[2])


def shifted_cots(cot_ref, later_ref):
    half = ROWS * W
    middle = jnp.concatenate([cot_ref[half:, :], later_ref[:half, :]], axis=0)
    return [cot_ref[...], middle, later_ref[...]]


def rows_at(block, low, high, offset):
    if offset == 0:
        return block[...].reshape(PIX, C)
    parts = []
    for frame in range(FRAMES):
        if offset < 0:
            parts += [low[frame], block[frame, 0]]
        else:
            parts += [block[frame, 1], high[frame]]
    return jnp.concatenate(parts, axis=0)


def put(core_ref, mine_ref, other_ref, block, start, value):
    first_core = core_ref[0] == 0
    value = value.astype(bf16)
    left, right = value[:, :, :128], value[:, :, 128:]
    count = value.shape[0]
    mine_ref[block, start : start + count] = jnp.where(first_core, left, right)
    other_ref[block, start : start + count] = jnp.where(first_core, right, left)


def paired(one, two):
    return jnp.concatenate([one.reshape(SPACES, 8, C), two.reshape(SPACES, 8, C)], axis=1)


def gradients_kernel(
    core_ref, in_ref, low_ref, high_ref, spatial_ref, act_grad_ref, cot_ref, later_cot_ref, up_ref,
    later_up_ref, time_ref, pre_ref, mine_ref, other_ref,
):
    half = ROWS * W
    taps = [None] * 3
    for i in range(3):
        rows = rows_at(in_ref, low_ref, high_ref, i - 1)
        for j in range(3):
            part = dot(rows, spatial_ref[i, j])
            taps[j] = part if taps[j] is None else taps[j] + part
    pre_act = from_left(taps[0]) + taps[1] + from_right(taps[2])
    scale = jnp.sqrt(jnp.mean(pre_act * pre_act, -1, keepdims=True) + epsilon)
    normed = pre_act / scale
    sig = 1.0 / (1.0 + jnp.exp(-normed))
    act = (normed / (1.0 + jnp.exp(-normed))).astype(bf16)
    act_grad = act_grad_ref[...]
    norm_grad = act_grad * sig * (1.0 + normed * (1.0 - sig))
    mean = jnp.mean(norm_grad * normed, -1, keepdims=True)
    pre = ((norm_grad - normed * mean) / scale).astype(bf16)
    pre_ref[...] = pre
    wide = pre.astype(f32)
    shifted = [from_right(wide).astype(bf16), pre, from_left(wide).astype(bf16)]

    cots = shifted_cots(cot_ref, later_cot_ref)

    def tap(at):
        if at < 9:
            return dot_at(shifted[at % 3], rows_at(in_ref, low_ref, high_ref, at // 3 - 1))
        return dot_at(cots[at - 9], act)

    for block in range(6):
        value = paired(tap(2 * block), tap(2 * block + 1))
        put(core_ref, mine_ref, other_ref, block, 0, value)
    own = in_ref[...].reshape(PIX, C)
    mixed = [
        (own.astype(f32) + dot(act, time_ref[0])).astype(bf16),
        dot(act, time_ref[1]).astype(bf16),
        dot(act, time_ref[2]).astype(bf16),
    ]
    for at in range(4):
        part = dot_at(up_ref[at], mixed[0])
        part = part + dot_at(up_ref[at, half:, :], mixed[1][:half, :])
        part = part + dot_at(later_up_ref[at, :half, :], mixed[1][half:, :])
        part = part + dot_at(later_up_ref[at], mixed[2])
        part = part.reshape(8, 32, C)
        for low in range(2):
            rows = part[:, low * 16 : low * 16 + 16]
            put(core_ref, mine_ref, other_ref, 6 + low, at * 8, rows)


def swap_sum_kernel(mine_ref, arrived_ref, out_ref, held_ref, sems):
    copies = []
    for at in range(8):
        total = (mine_ref[at] + arrived_ref[at]).reshape(2, 8, 2, 16, 128)
        for low in range(2):
            held_ref[at, :, low] = total[:, :, low]
        copies.append(pltpu.make_async_copy(held_ref.at[at], out_ref.at[at], sems.at[at]))
        copies[-1].start()
    for copy in copies:
        copy.wait()


def total_of(parts_ref):
    total = parts_ref[0].astype(f32)
    for at in range(1, parts_ref.shape[0]):
        total = total + parts_ref[at].astype(f32)
    return total


def near_sum_kernel(parts_ref, out_ref):
    out_ref[...] = total_of(parts_ref).astype(bf16)


def far_sum_kernel(parts_ref, out_ref):
    total = total_of(parts_ref)
    for at in range(MEMBERS):
        out_ref[at] = total


def input_grad_kernel(state_ref, pre_ref, low_ref, high_ref, weight_ref, out_ref):
    taps = [None] * 3
    for i in range(3):
        rows = rows_at(pre_ref, low_ref, high_ref, 1 - i)
        for j in range(3):
            part = dot_bt(rows, weight_ref[i, j])
            taps[j] = part if taps[j] is None else taps[j] + part
    total = state_ref[...] + (from_right(taps[0]) + taps[1] + from_left(taps[2]))
    out_ref[...] = total.astype(bf16)


def unpack_kernel(in_ref, spatial_ref, time_ref, up_ref):
    for block in range(6):
        for lane in range(2):
            for low in range(2):
                at = 2 * block + low
                value = in_ref[2 * block + lane, low * 8 : low * 8 + 8, :]
                if at < 9:
                    spatial_ref[at, :, lane * 128 : lane * 128 + 128] = value
                else:
                    time_ref[at - 9, :, lane * 128 : lane * 128 + 128] = value
    for low in range(2):
        for lane in range(2):
            up_ref[low * 16 : low * 16 + 16, lane * 128 : lane * 128 + 128] = in_ref[
                12 + 2 * low + lane
            ]


def own_upward(cotangent):
    return call(own_kernel, (shape((4, PIX, C), bf16),), 2 * PIX * C * C, cotangent)[0]


def states(*operands):
    wide, flat = shape((PIX, C), f32), shape((PIX, C), bf16)
    outs = (shape((4, PIX, C), bf16), wide, wide, flat, flat)
    return call(state_kernel, outs, 24 * PIX * C * C, *operands)


def gradients(*operands):
    half = shape((8, SPACES, 16, 128), bf16)
    specs = with_scalars(operands)
    outs = (shape((PIX, C), bf16), half, half)
    return call(gradients_kernel, outs, 76 * PIX * C * C, *operands, in_specs=specs)


def swap_sum(*operands):
    out = shape((8, 2, 2, 8, 16, 128), bf16)
    return call(
        swap_sum_kernel,
        out,
        0,
        *operands,
        out_specs=pl.BlockSpec(memory_space=pl.ANY),
        scratch_shapes=[pltpu.VMEM(out.shape, bf16), pltpu.SemaphoreType.DMA((8,))],
    )


def input_gradient(*operands):
    outs = (shape((PIX, C), bf16),)
    return call(input_grad_kernel, outs, 18 * PIX * C * C, *operands)[0]


def unpacked(gathered):
    outs = (shape((9, 8, C), f32), shape((3, 8, C), f32), shape((32, C), f32))
    return call(unpack_kernel, outs, 0, gathered)


def halo(block, after):
    even = (lax.axis_index(SPACE) & 1) == 0
    top, bottom = block[:, 0], block[:, ROWS - 1]
    pairs = [[(i, i + 1) for i in range(start, SPACES - 1, 2)] for start in (0, 1)]
    pairs = [found + [(b, a) for a, b in found] for found in pairs]
    first = lax.ppermute(jnp.where(even, bottom, top), SPACE, pairs[0])
    second = lax.ppermute(jnp.where(even, top, bottom), SPACE, pairs[1])
    first, second, after = lax.optimization_barrier((first, second, after))
    return jnp.where(even, second, first), jnp.where(even, first, second), after


def local(inputs, cotangent, spatial_weight, time_weight, up_weight):
    tile = inputs.reshape(FRAMES, ROWS, W, C)
    cotangent = cotangent.reshape(2 * FRAMES, 2 * ROWS, 2 * W, -1)
    later = lax.ppermute(cotangent, TIME, [(i + 1, i) for i in range(7)])
    upward = own_upward(cotangent)
    later, upward = lax.optimization_barrier((later, upward))
    later_up, state_grad, act_grad, time_cot, later_cot = states(
        later, upward, up_weight, time_weight
    )
    low, high, later_cot = halo(tile, later_cot)
    core = lax.axis_index("core").astype(jnp.int32).reshape(1)
    pre_grad, mine, other = gradients(
        core, tile, low, high, spatial_weight, act_grad, time_cot, later_cot, upward, later_up,
        time_weight,
    )
    other = lax.ppermute(other, "core", [(0, 1), (1, 0)])
    value = swap_sum(mine, other)
    pre_tile = pre_grad.reshape(FRAMES, ROWS, W, C)
    held, value = lax.optimization_barrier((pre_tile, value))
    value = lax.all_to_all(value.reshape(32, 8, 16, 128), NEAR, 0, 0)
    pre_low, pre_high, state_grad = halo(held, state_grad)
    input_grad = input_gradient(state_grad, pre_tile, pre_low, pre_high, spatial_weight)
    value = call(near_sum_kernel, (shape((8, 16, 128), bf16),), 0, value)[0]
    value = lax.all_to_all(value, "z_hi", 0, 0)
    value, input_grad = lax.optimization_barrier((value, input_grad))
    value = call(far_sum_kernel, (shape((MEMBERS, 16, 128), f32),), 0, value)[0]
    spatial_grad, time_grad, up_grad = unpacked(lax.all_to_all(value, GROUP, 0, 0))
    return (
        input_grad.reshape(inputs.shape),
        jnp.swapaxes(spatial_grad.reshape(3, 3, 8, C), 2, 3),
        jnp.swapaxes(time_grad, 1, 2),
        jnp.swapaxes(up_grad, 0, 1),
    )


def solution(mesh):
    whole = Mesh(
        mesh.devices.reshape(2, 4, 2, 2, 8, 2), ("y_lo", "x", "core", "y_hi", "z_hi", "z_lo")
    )
    tile = P("y_lo", TIME, SPACE, None, None)
    return jax.shard_map(
        local,
        mesh=whole,
        in_specs=(tile, tile, P(), P(), P()),
        out_specs=(tile, P(None, None, None, SPACE), P(None, None, SPACE), P(None, SPACE)),
        check_vma=False,
    )
```

```python
import jax
import jax.numpy as jnp
from jax import lax
from jax.experimental import pallas as pl
from jax.experimental.pallas import tpu as pltpu
from jax.sharding import Mesh, PartitionSpec as P

epsilon = 1e-06
TIME = ("x", "core")
SPACE = ("y_hi", "z_hi", "z_lo")
GROUP = ("y_lo", "x", "core")
NEAR = ("y_lo", "x", "y_hi", "z_lo")
C = 256
W = 64
FRAMES = 2
ROWS = 2
PIX = FRAMES * ROWS * W
SPACES = 32
MEMBERS = 16
bf16 = jnp.bfloat16
f32 = jnp.float32


def dot(a, b):
    return lax.dot_general(a, b, (((1,), (0,)), ((), ())), preferred_element_type=f32)


def dot_bt(a, b):
    return lax.dot_general(a, b, (((1,), (1,)), ((), ())), preferred_element_type=f32)


def dot_at(a, b):
    return lax.dot_general(a, b, (((0,), (0,)), ((), ())), preferred_element_type=f32)


def column():
    return lax.broadcasted_iota(jnp.int32, (PIX, C), 0) & (W - 1)


def from_left(value):
    return jnp.where(column() == 0, 0.0, pltpu.roll(value, 1, 0))


def from_right(value):
    return jnp.where(column() == W - 1, 0.0, pltpu.roll(value, PIX - 1, 0))


def call(kernel, outs, flops, *operands, **given):
    moved = sum(v.size * v.dtype.itemsize for v in operands)
    moved += sum(s.size * s.dtype.itemsize for s in jax.tree.leaves(outs))
    return pl.pallas_call(
        kernel,
        out_shape=outs,
        compiler_params=pltpu.CompilerParams(vmem_limit_bytes=40 << 20),
        cost_estimate=pl.CostEstimate(flops=flops, bytes_accessed=moved, transcendentals=0),
        **given,
    )(*operands)


def with_scalars(operands):
    specs = [pl.BlockSpec(memory_space=pltpu.SMEM)]
    return specs + [pl.BlockSpec(memory_space=pltpu.VMEM)] * (len(operands) - 1)


def shape(dims, dtype):
    return jax.ShapeDtypeStruct(dims, dtype)


def arranged(cot_ref, up_ref):
    row = lax.broadcasted_iota(jnp.int32, (2 * W, 2 * W), 0)
    col = lax.broadcasted_iota(jnp.int32, (2 * W, 2 * W), 1)
    order = (col == 2 * (row & (W - 1)) + (row >> 6)).astype(f32).astype(bf16)
    for frame in range(FRAMES):
        for height in range(ROWS):
            first = (frame * ROWS + height) * W
            for t in range(2):
                pair = jnp.concatenate(
                    [cot_ref[2 * frame + t, 2 * height + p] for p in range(2)], axis=1
                )
                pair = dot(order, pair).astype(bf16)
                for p in range(2):
                    for q in range(2):
                        up_ref[2 * t + p, first : first + W, q * 128 : q * 128 + 128] = pair[
                            q * W : q * W + W, p * 128 : p * 128 + 128
                        ]


def state_of(up_ref, weight_ref):
    state = None
    for at in range(4):
        part = dot_bt(up_ref[at], weight_ref[:, at * C : at * C + C])
        state = part if state is None else state + part
    return state


def own_kernel(cot_ref, up_ref):
    arranged(cot_ref, up_ref)


def state_kernel(
    cot_ref, up_ref, weight_ref, later_up_ref, state_ref, time_cot_ref, later_cot_ref
):
    state = state_of(up_ref, weight_ref)
    state_ref[...] = state
    time_cot_ref[...] = state.astype(bf16)
    arranged(cot_ref, later_up_ref)
    later_cot_ref[...] = state_of(later_up_ref, weight_ref).astype(bf16)


def rows_at(block, low, high, offset):
    if offset == 0:
        return block[...].reshape(PIX, C)
    parts = []
    for frame in range(FRAMES):
        if offset < 0:
            parts += [low[frame], block[frame, 0]]
        else:
            parts += [block[frame, 1], high[frame]]
    return jnp.concatenate(parts, axis=0)


def put(core_ref, mine_ref, other_ref, block, start, value):
    first_core = core_ref[0] == 0
    value = value.astype(bf16)
    left, right = value[:, :, :128], value[:, :, 128:]
    count = value.shape[0]
    mine_ref[block, start : start + count] = jnp.where(first_core, left, right)
    other_ref[block, start : start + count] = jnp.where(first_core, right, left)


def paired(one, two):
    return jnp.concatenate([one.reshape(SPACES, 8, C), two.reshape(SPACES, 8, C)], axis=1)


def gradients_kernel(
    core_ref, in_ref, low_ref, high_ref, spatial_ref, cot_ref, later_cot_ref, up_ref, later_up_ref,
    time_ref, pre_ref, mine_ref, other_ref,
):
    half = ROWS * W
    taps = [None] * 3
    for i in range(3):
        rows = rows_at(in_ref, low_ref, high_ref, i - 1)
        for j in range(3):
            part = dot(rows, spatial_ref[i, j])
            taps[j] = part if taps[j] is None else taps[j] + part
    pre_act = from_left(taps[0]) + taps[1] + from_right(taps[2])
    scale = jnp.sqrt(jnp.mean(pre_act * pre_act, -1, keepdims=True) + epsilon)
    normed = pre_act / scale
    sig = 1.0 / (1.0 + jnp.exp(-normed))
    act = (normed / (1.0 + jnp.exp(-normed))).astype(bf16)
    middle = jnp.concatenate([cot_ref[half:, :], later_cot_ref[:half, :]], axis=0)
    act_grad = dot_bt(cot_ref[...], time_ref[0]) + dot_bt(middle, time_ref[1])
    act_grad = act_grad + dot_bt(later_cot_ref[...], time_ref[2])
    norm_grad = act_grad * sig * (1.0 + normed * (1.0 - sig))
    mean = jnp.mean(norm_grad * normed, -1, keepdims=True)
    pre = ((norm_grad - normed * mean) / scale).astype(bf16)
    pre_ref[...] = pre
    wide = pre.astype(f32)
    shifted = [from_right(wide).astype(bf16), pre, from_left(wide).astype(bf16)]

    cots = [cot_ref[...], middle, later_cot_ref[...]]

    def tap(at):
        if at < 9:
            return dot_at(shifted[at % 3], rows_at(in_ref, low_ref, high_ref, at // 3 - 1))
        return dot_at(cots[at - 9], act)

    for block in range(6):
        value = paired(tap(2 * block), tap(2 * block + 1))
        put(core_ref, mine_ref, other_ref, block, 0, value)
    own = in_ref[...].reshape(PIX, C)
    mixed = [
        (own.astype(f32) + dot(act, time_ref[0])).astype(bf16),
        dot(act, time_ref[1]).astype(bf16),
        dot(act, time_ref[2]).astype(bf16),
    ]
    for at in range(4):
        part = dot_at(up_ref[at], mixed[0])
        part = part + dot_at(up_ref[at, half:, :], mixed[1][:half, :])
        part = part + dot_at(later_up_ref[at, :half, :], mixed[1][half:, :])
        part = part + dot_at(later_up_ref[at], mixed[2])
        part = part.reshape(8, 32, C)
        for low in range(2):
            rows = part[:, low * 16 : low * 16 + 16]
            put(core_ref, mine_ref, other_ref, 6 + low, at * 8, rows)


def swap_sum_kernel(mine_ref, arrived_ref, out_ref, held_ref, sems):
    copies = []
    for at in range(8):
        total = (mine_ref[at] + arrived_ref[at]).reshape(2, 8, 2, 16, 128)
        for low in range(2):
            held_ref[at, :, low] = total[:, :, low]
        copies.append(pltpu.make_async_copy(held_ref.at[at], out_ref.at[at], sems.at[at]))
        copies[-1].start()
    for copy in copies:
        copy.wait()


def total_of(parts_ref):
    total = parts_ref[0].astype(f32)
    for at in range(1, parts_ref.shape[0]):
        total = total + parts_ref[at].astype(f32)
    return total


def near_sum_kernel(parts_ref, out_ref):
    out_ref[...] = total_of(parts_ref).astype(bf16)


def far_sum_kernel(parts_ref, out_ref):
    total = total_of(parts_ref)
    for at in range(MEMBERS):
        out_ref[at] = total


def input_grad_kernel(state_ref, pre_ref, low_ref, high_ref, weight_ref, out_ref):
    taps = [None] * 3
    for i in range(3):
        rows = rows_at(pre_ref, low_ref, high_ref, 1 - i)
        for j in range(3):
            part = dot_bt(rows, weight_ref[i, j])
            taps[j] = part if taps[j] is None else taps[j] + part
    total = state_ref[...] + (from_right(taps[0]) + taps[1] + from_left(taps[2]))
    out_ref[...] = total.astype(bf16)


def unpack_kernel(in_ref, spatial_ref, time_ref, up_ref):
    for block in range(6):
        for lane in range(2):
            for low in range(2):
                at = 2 * block + low
                value = in_ref[2 * block + lane, low * 8 : low * 8 + 8, :]
                if at < 9:
                    spatial_ref[at, :, lane * 128 : lane * 128 + 128] = value
                else:
                    time_ref[at - 9, :, lane * 128 : lane * 128 + 128] = value
    for low in range(2):
        for lane in range(2):
            up_ref[low * 16 : low * 16 + 16, lane * 128 : lane * 128 + 128] = in_ref[
                12 + 2 * low + lane
            ]


def own_upward(cotangent):
    return call(own_kernel, (shape((4, PIX, C), bf16),), 2 * PIX * C * C, cotangent)[0]


def states(later, upward, up_weight):
    flat = shape((PIX, C), bf16)
    outs = (shape((4, PIX, C), bf16), shape((PIX, C), f32), flat, flat)
    return call(state_kernel, outs, 18 * PIX * C * C, later, upward, up_weight)


def gradients(*operands):
    half = shape((8, SPACES, 16, 128), bf16)
    specs = with_scalars(operands)
    outs = (shape((PIX, C), bf16), half, half)
    return call(gradients_kernel, outs, 76 * PIX * C * C, *operands, in_specs=specs)


def swap_sum(*operands):
    out = shape((8, 2, 2, 8, 16, 128), bf16)
    return call(
        swap_sum_kernel,
        out,
        0,
        *operands,
        out_specs=pl.BlockSpec(memory_space=pl.ANY),
        scratch_shapes=[pltpu.VMEM(out.shape, bf16), pltpu.SemaphoreType.DMA((8,))],
    )


def input_gradient(*operands):
    outs = (shape((PIX, C), bf16),)
    return call(input_grad_kernel, outs, 18 * PIX * C * C, *operands)[0]


def unpacked(gathered):
    outs = (shape((9, 8, C), f32), shape((3, 8, C), f32), shape((32, C), f32))
    return call(unpack_kernel, outs, 0, gathered)


def halo(block, after):
    even = (lax.axis_index(SPACE) & 1) == 0
    top, bottom = block[:, 0], block[:, ROWS - 1]
    pairs = [[(i, i + 1) for i in range(start, SPACES - 1, 2)] for start in (0, 1)]
    pairs = [found + [(b, a) for a, b in found] for found in pairs]
    first = lax.ppermute(jnp.where(even, bottom, top), SPACE, pairs[0])
    second = lax.ppermute(jnp.where(even, top, bottom), SPACE, pairs[1])
    first, second, after = lax.optimization_barrier((first, second, after))
    return jnp.where(even, second, first), jnp.where(even, first, second), after


def local(inputs, cotangent, spatial_weight, time_weight, up_weight):
    tile = inputs.reshape(FRAMES, ROWS, W, C)
    cotangent = cotangent.reshape(2 * FRAMES, 2 * ROWS, 2 * W, -1)
    later = lax.ppermute(cotangent, TIME, [(i + 1, i) for i in range(7)])
    upward = own_upward(cotangent)
    later, upward = lax.optimization_barrier((later, upward))
    later_up, state_grad, time_cot, later_cot = states(later, upward, up_weight)
    low, high, later_cot = halo(tile, later_cot)
    core = lax.axis_index("core").astype(jnp.int32).reshape(1)
    pre_grad, mine, other = gradients(
        core, tile, low, high, spatial_weight, time_cot, later_cot, upward, later_up, time_weight
    )
    other = lax.ppermute(other, "core", [(0, 1), (1, 0)])
    value = swap_sum(mine, other)
    pre_tile = pre_grad.reshape(FRAMES, ROWS, W, C)
    value = lax.all_to_all(value.reshape(32, 8, 16, 128), NEAR, 0, 0)
    value = call(near_sum_kernel, (shape((8, 16, 128), bf16),), 0, value)[0]
    held, value = lax.optimization_barrier((pre_tile, value))
    value = lax.all_to_all(value, "z_hi", 0, 0)
    pre_low, pre_high, state_grad = halo(held, state_grad)
    input_grad = input_gradient(state_grad, pre_tile, pre_low, pre_high, spatial_weight)
    value, input_grad = lax.optimization_barrier((value, input_grad))
    value = call(far_sum_kernel, (shape((MEMBERS, 16, 128), f32),), 0, value)[0]
    spatial_grad, time_grad, up_grad = unpacked(lax.all_to_all(value, GROUP, 0, 0))
    return (
        input_grad.reshape(inputs.shape),
        jnp.swapaxes(spatial_grad.reshape(3, 3, 8, C), 2, 3),
        jnp.swapaxes(time_grad, 1, 2),
        jnp.swapaxes(up_grad, 0, 1),
    )


def solution(mesh):
    whole = Mesh(
        mesh.devices.reshape(2, 4, 2, 2, 8, 2), ("y_lo", "x", "core", "y_hi", "z_hi", "z_lo")
    )
    tile = P("y_lo", TIME, SPACE, None, None)
    return jax.shard_map(
        local,
        mesh=whole,
        in_specs=(tile, tile, P(), P(), P()),
        out_specs=(tile, P(None, None, None, SPACE), P(None, None, SPACE), P(None, SPACE)),
        check_vma=False,
    )
```

```python
import jax
import jax.numpy as jnp
from jax import lax
from jax.experimental import pallas as pl
from jax.experimental.pallas import tpu as pltpu
from jax.sharding import Mesh, PartitionSpec as P

epsilon = 1e-06
TIME = ("x", "core")
SPACE = ("y_hi", "z_hi", "z_lo")
GROUP = ("y_lo", "x", "core")
NEAR = ("z_lo", "y_hi", "y_lo", "x")
C = 256
W = 64
FRAMES = 2
ROWS = 2
PIX = FRAMES * ROWS * W
SPACES = 32
MEMBERS = 16
bf16 = jnp.bfloat16
f32 = jnp.float32


def dot(a, b):
    return lax.dot_general(a, b, (((1,), (0,)), ((), ())), preferred_element_type=f32)


def dot_bt(a, b):
    return lax.dot_general(a, b, (((1,), (1,)), ((), ())), preferred_element_type=f32)


def dot_at(a, b):
    return lax.dot_general(a, b, (((0,), (0,)), ((), ())), preferred_element_type=f32)


def column():
    return lax.broadcasted_iota(jnp.int32, (PIX, C), 0) & (W - 1)


def from_left(value):
    return jnp.where(column() == 0, 0.0, pltpu.roll(value, 1, 0))


def from_right(value):
    return jnp.where(column() == W - 1, 0.0, pltpu.roll(value, PIX - 1, 0))


def call(kernel, outs, flops, *operands, **given):
    moved = sum(v.size * v.dtype.itemsize for v in operands)
    moved += sum(s.size * s.dtype.itemsize for s in jax.tree.leaves(outs))
    return pl.pallas_call(
        kernel,
        out_shape=outs,
        compiler_params=pltpu.CompilerParams(vmem_limit_bytes=40 << 20),
        cost_estimate=pl.CostEstimate(flops=flops, bytes_accessed=moved, transcendentals=0),
        **given,
    )(*operands)


def with_scalars(operands):
    specs = [pl.BlockSpec(memory_space=pltpu.SMEM)]
    return specs + [pl.BlockSpec(memory_space=pltpu.VMEM)] * (len(operands) - 1)


def shape(dims, dtype):
    return jax.ShapeDtypeStruct(dims, dtype)


def arranged(cot_ref, up_ref):
    row = lax.broadcasted_iota(jnp.int32, (2 * W, 2 * W), 0)
    col = lax.broadcasted_iota(jnp.int32, (2 * W, 2 * W), 1)
    order = (col == 2 * (row & (W - 1)) + (row >> 6)).astype(f32).astype(bf16)
    for frame in range(FRAMES):
        for height in range(ROWS):
            first = (frame * ROWS + height) * W
            for t in range(2):
                pair = jnp.concatenate(
                    [cot_ref[2 * frame + t, 2 * height + p] for p in range(2)], axis=1
                )
                pair = dot(order, pair).astype(bf16)
                for p in range(2):
                    for q in range(2):
                        up_ref[2 * t + p, first : first + W, q * 128 : q * 128 + 128] = pair[
                            q * W : q * W + W, p * 128 : p * 128 + 128
                        ]


def state_of(up_ref, weight_ref):
    state = None
    for at in range(4):
        part = dot_bt(up_ref[at], weight_ref[:, at * C : at * C + C])
        state = part if state is None else state + part
    return state


def own_kernel(cot_ref, up_ref):
    arranged(cot_ref, up_ref)


def state_kernel(
    cot_ref, up_ref, weight_ref, later_up_ref, state_ref, time_cot_ref, later_cot_ref
):
    state = state_of(up_ref, weight_ref)
    state_ref[...] = state
    time_cot_ref[...] = state.astype(bf16)
    arranged(cot_ref, later_up_ref)
    later_cot_ref[...] = state_of(later_up_ref, weight_ref).astype(bf16)


def rows_at(block, low, high, offset):
    if offset == 0:
        return block[...].reshape(PIX, C)
    parts = []
    for frame in range(FRAMES):
        if offset < 0:
            parts += [low[frame], block[frame, 0]]
        else:
            parts += [block[frame, 1], high[frame]]
    return jnp.concatenate(parts, axis=0)


def put(core_ref, mine_ref, other_ref, block, start, value):
    first_core = core_ref[0] == 0
    value = value.astype(bf16)
    left, right = value[:, :, :128], value[:, :, 128:]
    count = value.shape[0]
    mine_ref[block, start : start + count] = jnp.where(first_core, left, right)
    other_ref[block, start : start + count] = jnp.where(first_core, right, left)


def paired(one, two):
    return jnp.concatenate([one.reshape(SPACES, 8, C), two.reshape(SPACES, 8, C)], axis=1)


def gradients_kernel(
    core_ref, in_ref, low_ref, high_ref, spatial_ref, cot_ref, later_cot_ref, up_ref, later_up_ref,
    time_ref, pre_ref, mine_ref, other_ref,
):
    half = ROWS * W
    taps = [None] * 3
    for i in range(3):
        rows = rows_at(in_ref, low_ref, high_ref, i - 1)
        for j in range(3):
            part = dot(rows, spatial_ref[i, j])
            taps[j] = part if taps[j] is None else taps[j] + part
    pre_act = from_left(taps[0]) + taps[1] + from_right(taps[2])
    scale = jnp.sqrt(jnp.mean(pre_act * pre_act, -1, keepdims=True) + epsilon)
    normed = pre_act / scale
    sig = 1.0 / (1.0 + jnp.exp(-normed))
    act = (normed / (1.0 + jnp.exp(-normed))).astype(bf16)
    middle = jnp.concatenate([cot_ref[half:, :], later_cot_ref[:half, :]], axis=0)
    act_grad = dot_bt(cot_ref[...], time_ref[0]) + dot_bt(middle, time_ref[1])
    act_grad = act_grad + dot_bt(later_cot_ref[...], time_ref[2])
    norm_grad = act_grad * sig * (1.0 + normed * (1.0 - sig))
    mean = jnp.mean(norm_grad * normed, -1, keepdims=True)
    pre = ((norm_grad - normed * mean) / scale).astype(bf16)
    pre_ref[...] = pre
    wide = pre.astype(f32)
    shifted = [from_right(wide).astype(bf16), pre, from_left(wide).astype(bf16)]

    cots = [cot_ref[...], middle, later_cot_ref[...]]

    def tap(at):
        if at < 9:
            return dot_at(shifted[at % 3], rows_at(in_ref, low_ref, high_ref, at // 3 - 1))
        return dot_at(cots[at - 9], act)

    for block in range(6):
        value = paired(tap(2 * block), tap(2 * block + 1))
        put(core_ref, mine_ref, other_ref, block, 0, value)
    own = in_ref[...].reshape(PIX, C)
    mixed = [
        (own.astype(f32) + dot(act, time_ref[0])).astype(bf16),
        dot(act, time_ref[1]).astype(bf16),
        dot(act, time_ref[2]).astype(bf16),
    ]
    for at in range(4):
        part = dot_at(up_ref[at], mixed[0])
        part = part + dot_at(up_ref[at, half:, :], mixed[1][:half, :])
        part = part + dot_at(later_up_ref[at, :half, :], mixed[1][half:, :])
        part = part + dot_at(later_up_ref[at], mixed[2])
        part = part.reshape(8, 32, C)
        for low in range(2):
            rows = part[:, low * 16 : low * 16 + 16]
            put(core_ref, mine_ref, other_ref, 6 + low, at * 8, rows)


def swap_sum_kernel(mine_ref, arrived_ref, out_ref, held_ref, sems):
    copies = []
    for at in range(8):
        total = (mine_ref[at] + arrived_ref[at]).reshape(2, 8, 2, 16, 128)
        for low in range(2):
            held_ref[at, low] = total[:, :, low]
        copies.append(pltpu.make_async_copy(held_ref.at[at], out_ref.at[:, :, at], sems.at[at]))
        copies[-1].start()
    for copy in copies:
        copy.wait()


def total_of(parts_ref):
    total = parts_ref[0].astype(f32)
    for at in range(1, parts_ref.shape[0]):
        total = total + parts_ref[at].astype(f32)
    return total


def near_sum_kernel(parts_ref, out_ref):
    out_ref[...] = total_of(parts_ref).astype(bf16)


def far_sum_kernel(parts_ref, out_ref):
    total = total_of(parts_ref)
    for at in range(MEMBERS):
        out_ref[at] = total


def input_grad_kernel(state_ref, pre_ref, low_ref, high_ref, weight_ref, out_ref):
    taps = [None] * 3
    for i in range(3):
        rows = rows_at(pre_ref, low_ref, high_ref, 1 - i)
        for j in range(3):
            part = dot_bt(rows, weight_ref[i, j])
            taps[j] = part if taps[j] is None else taps[j] + part
    total = state_ref[...] + (from_right(taps[0]) + taps[1] + from_left(taps[2]))
    out_ref[...] = total.astype(bf16)


def unpack_kernel(in_ref, spatial_ref, time_ref, up_ref):
    for block in range(6):
        for lane in range(2):
            for low in range(2):
                at = 2 * block + low
                value = in_ref[2 * block + lane, low * 8 : low * 8 + 8, :]
                if at < 9:
                    spatial_ref[at, :, lane * 128 : lane * 128 + 128] = value
                else:
                    time_ref[at - 9, :, lane * 128 : lane * 128 + 128] = value
    for low in range(2):
        for lane in range(2):
            up_ref[low * 16 : low * 16 + 16, lane * 128 : lane * 128 + 128] = in_ref[
                12 + 2 * low + lane
            ]


def own_upward(cotangent):
    return call(own_kernel, (shape((4, PIX, C), bf16),), 2 * PIX * C * C, cotangent)[0]


def states(later, upward, up_weight):
    flat = shape((PIX, C), bf16)
    outs = (shape((4, PIX, C), bf16), shape((PIX, C), f32), flat, flat)
    return call(state_kernel, outs, 18 * PIX * C * C, later, upward, up_weight)


def gradients(*operands):
    half = shape((8, SPACES, 16, 128), bf16)
    specs = with_scalars(operands)
    outs = (shape((PIX, C), bf16), half, half)
    return call(gradients_kernel, outs, 76 * PIX * C * C, *operands, in_specs=specs)


def swap_sum(*operands):
    out = shape((2, 2, 8, 8, 16, 128), bf16)
    return call(
        swap_sum_kernel,
        out,
        0,
        *operands,
        out_specs=pl.BlockSpec(memory_space=pl.ANY),
        scratch_shapes=[
            pltpu.VMEM((8, 2, 2, 8, 16, 128), bf16), pltpu.SemaphoreType.DMA((8,))
        ],
    )


def input_gradient(*operands):
    outs = (shape((PIX, C), bf16),)
    return call(input_grad_kernel, outs, 18 * PIX * C * C, *operands)[0]


def unpacked(gathered):
    outs = (shape((9, 8, C), f32), shape((3, 8, C), f32), shape((32, C), f32))
    return call(unpack_kernel, outs, 0, gathered)


def halo(block, after):
    even = (lax.axis_index(SPACE) & 1) == 0
    top, bottom = block[:, 0], block[:, ROWS - 1]
    pairs = [[(i, i + 1) for i in range(start, SPACES - 1, 2)] for start in (0, 1)]
    pairs = [found + [(b, a) for a, b in found] for found in pairs]
    first = lax.ppermute(jnp.where(even, bottom, top), SPACE, pairs[0])
    second = lax.ppermute(jnp.where(even, top, bottom), SPACE, pairs[1])
    first, second, after = lax.optimization_barrier((first, second, after))
    return jnp.where(even, second, first), jnp.where(even, first, second), after


def local(inputs, cotangent, spatial_weight, time_weight, up_weight):
    tile = inputs.reshape(FRAMES, ROWS, W, C)
    cotangent = cotangent.reshape(2 * FRAMES, 2 * ROWS, 2 * W, -1)
    later = lax.ppermute(cotangent, TIME, [(i + 1, i) for i in range(7)])
    upward = own_upward(cotangent)
    later, upward = lax.optimization_barrier((later, upward))
    later_up, state_grad, time_cot, later_cot = states(later, upward, up_weight)
    low, high, later_cot = halo(tile, later_cot)
    core = lax.axis_index("core").astype(jnp.int32).reshape(1)
    pre_grad, mine, other = gradients(
        core, tile, low, high, spatial_weight, time_cot, later_cot, upward, later_up, time_weight
    )
    other = lax.ppermute(other, "core", [(0, 1), (1, 0)])
    value = swap_sum(mine, other)
    pre_tile = pre_grad.reshape(FRAMES, ROWS, W, C)
    held, value = lax.optimization_barrier((pre_tile, value))
    value = lax.all_to_all(value.reshape(32, 8, 16, 128), NEAR, 0, 0)
    pre_low, pre_high, state_grad = halo(held, state_grad)
    input_grad = input_gradient(state_grad, pre_tile, pre_low, pre_high, spatial_weight)
    value, input_grad = lax.optimization_barrier((value, input_grad))
    value = call(near_sum_kernel, (shape((8, 16, 128), bf16),), 0, value)[0]
    value = lax.all_to_all(value, "z_hi", 0, 0)
    value = call(far_sum_kernel, (shape((MEMBERS, 16, 128), f32),), 0, value)[0]
    spatial_grad, time_grad, up_grad = unpacked(lax.all_to_all(value, GROUP, 0, 0))
    return (
        input_grad.reshape(inputs.shape),
        jnp.swapaxes(spatial_grad.reshape(3, 3, 8, C), 2, 3),
        jnp.swapaxes(time_grad, 1, 2),
        jnp.swapaxes(up_grad, 0, 1),
    )


def solution(mesh):
    whole = Mesh(
        mesh.devices.reshape(2, 4, 2, 2, 8, 2), ("y_lo", "x", "core", "y_hi", "z_hi", "z_lo")
    )
    tile = P("y_lo", TIME, SPACE, None, None)
    return jax.shard_map(
        local,
        mesh=whole,
        in_specs=(tile, tile, P(), P(), P()),
        out_specs=(tile, P(None, None, None, SPACE), P(None, None, SPACE), P(None, SPACE)),
        check_vma=False,
    )
```
